768 devices in a mesh: reg: 12 (over z), blk: 64 (over y, x, core).
Axes of the slice: x: 4, y: 8, z: 12, core: 2. Of those that a mesh axis runs over, the one named last changes fastest.
Arguments:
- assembly_rhs: float32 [12, 640, 320], P('reg', 'blk'), may hold values from -250 to 250
- source_slot: int32 [12, 384], P('reg', 'blk'), may hold values from 0 to 639, as said below
- diagonal_blocks: float32 [12, 384, 320, 320], P('reg', 'blk'), may hold values from -2.5 to 2.5
- jacobi_blocks: bfloat16 [12, 384, 320, 320], P('reg', 'blk'), may hold values from -1.5 to 1.5
- coupling: float32 [12, 384, 6, 80, 80], P('reg', 'blk'), may hold values from -0.3125 to 0.3125
- neighbor: int32 [384, 4], P('blk'), may hold values from 0 to 383, as said below
- neighbor_face: int32 [384, 4], P('blk'), may hold values from 0 to 3, as said below
- orientation: int32 [384, 4], P('blk'), may hold values from 0 to 1
Outputs:
- solution: float32 [12, 384, 320], P('reg', 'blk')
- residual: float32 [12, 384, 320], P('reg', 'blk')
The draws below stay inside these ranges and needn't reach their ends.
Inputs may be any that keep to these rules, and one draw needn't show every extreme that they name: `source_slot`: within one layer the slots are distinct. The elements of one solver device come from at most 2 slots of any one assembly device, and this is reached; some assembly device holds 10 used slots. `neighbor`: the layer is a periodic quadrilateral mesh extruded across layers; the neighbour relation is symmetric. The side faces of one device's elements have neighbours on any one other device at most 3 times. `neighbor_face`: consistent with neighbor: the neighbour's face across face f faces back to this element.
All inputs are finite; a program needn't handle non-finite values.
Results may differ from the reference program's by a relative error of at most 0.0091.
Values sent between devices are 32-bit elements; how exact they have to be, the bound alone decides.
No kernel may reach another device: no remote copies, remote signals or barrier semaphores. Data moves between devices by JAX's collectives and lax.ppermute only.
A program may use at most 32 MiB of HBM per device.

```python
import math
import jax
import jax.numpy as jnp
from jax import lax

NVAR = 5
NQ = 4
DOF = 320
FDOF = 80
ELEM_DEV = 6
ASM_CAP = 10
KRYLOV = 2
REGIONS = 12
RANKS = 64
ELEM_REG = 384
ASM_SLOTS = 640


def adjacency(key):
    key = jax.random.fold_in(key, 101)
    tile_key, flip_key = jax.random.split(key)
    tiles_x = RANKS // 8
    cells_x = 2 * tiles_x
    cells_y = 24
    cell_x = jnp.repeat(jnp.arange(cells_x, dtype=jnp.int32), cells_y)
    cell_y = jnp.tile(jnp.arange(cells_y, dtype=jnp.int32), cells_x)
    tile_order = jax.random.permutation(tile_key, RANKS).astype(jnp.int32)
    device_of = tile_order[cell_x // 2 * 8 + cell_y // 3]
    element_of = device_of * ELEM_DEV + cell_x % 2 * 3 + cell_y % 3
    flips = jax.random.randint(flip_key, (2, cells_x * cells_y), 0, 2).astype(jnp.int32)
    flip_x, flip_y = (flips[0], flips[1])
    total = RANKS * ELEM_DEV
    near_table = jnp.zeros((total, 4), jnp.int32)
    face_table = jnp.zeros((total, 4), jnp.int32)
    turn_table = jnp.zeros((total, 4), jnp.int32)
    moves = ((-1, 0), (1, 0), (0, -1), (0, 1))
    for direction in range(4):
        step_x, step_y = moves[direction]
        other_x = (cell_x + step_x) % cells_x
        other_y = (cell_y + step_y) % cells_y
        other_cell = other_x * cells_y + other_y
        other_element = element_of[other_cell]
        lower = direction % 2
        if direction < 2:
            my_face = jnp.where(flip_x == 0, lower, 1 - lower)
            its_face = jnp.where(flip_x[other_cell] == 0, 1 - lower, lower)
            turned = flip_y ^ flip_y[other_cell]
        else:
            my_face = 2 + jnp.where(flip_y == 0, lower, 1 - lower)
            its_face = 2 + jnp.where(flip_y[other_cell] == 0, 1 - lower, lower)
            turned = flip_x ^ flip_x[other_cell]
        near_table = near_table.at[element_of, my_face].set(other_element)
        face_table = face_table.at[element_of, my_face].set(its_face)
        turn_table = turn_table.at[element_of, my_face].set(turned)
    return (near_table, face_table, turn_table)


def draw_neighbor(key, part):
    return adjacency(key)[0]


def draw_neighbor_face(key, part):
    return adjacency(key)[1]


def draw_orientation(key, part):
    return adjacency(key)[2]


def draw_source_slot(key, part):
    key = jax.random.fold_in(key, 11)

    def one_layer(layer_key):
        order_key, shuffle_key = jax.random.split(layer_key)
        device_order = jax.random.permutation(order_key, RANKS).astype(jnp.int32)
        shuffles = jax.vmap(lambda one_key: jax.random.permutation(one_key, ASM_CAP))(jax.random.split(shuffle_key, RANKS)).astype(jnp.int32)
        devices = jnp.arange(RANKS * ELEM_DEV, dtype=jnp.int32) // ELEM_DEV
        within = jnp.arange(RANKS * ELEM_DEV, dtype=jnp.int32) % ELEM_DEV
        quarter = devices % 4
        hub = devices - quarter
        source = jnp.where(within < 2, devices, jnp.where(within < 4, (devices + 1) % RANKS, jnp.where(quarter == 0, (devices + 2) % RANKS, hub)))
        place = jnp.where((within < 4) | (quarter == 0), within, 4 + 2 * (quarter - 1) + (within - 4))
        return device_order[source] * ASM_CAP + shuffles[source, place]
    return jax.vmap(one_layer)(jax.random.split(key, REGIONS)).astype(jnp.int32)


def draw_assembly_rhs(key, part):
    key = jax.random.fold_in(key, 7)
    base_key, scale_key = jax.random.split(key)
    shape = (REGIONS, ASM_SLOTS, DOF)
    position = (jnp.arange(REGIONS)[:, None] * ASM_SLOTS + jnp.arange(ASM_SLOTS)[None, :]).astype(jnp.float32)
    ramp = 1.0 + 2.0 * position / (REGIONS * ASM_SLOTS - 1)
    spread = jnp.exp(jax.random.uniform(scale_key, (REGIONS, ASM_SLOTS), minval=0.0, maxval=math.log(10.0)))
    values = jnp.clip(jax.random.normal(base_key, shape), -6.0, 6.0)
    return (values * (ramp * spread)[:, :, None]).astype(jnp.float32)


def dominant(centre_key, noise, low, high):
    centre = jax.random.uniform(centre_key, (REGIONS, ELEM_REG, DOF), minval=low, maxval=high)
    return noise + jnp.eye(DOF, dtype=jnp.float32) * centre[..., None]


def draw_diagonal_blocks(key, part):
    key = jax.random.fold_in(key, 3)
    centre_key, noise_key = jax.random.split(key)
    shape = (REGIONS, ELEM_REG, DOF, DOF)
    noise = jnp.clip(jax.random.normal(noise_key, shape), -4.0, 4.0)
    return dominant(centre_key, noise * (0.5 / math.sqrt(DOF)), 1.0, 2.0).astype(jnp.float32)


def draw_jacobi_blocks(key, part):
    key = jax.random.fold_in(key, 5)
    centre_key, noise_key = jax.random.split(key)
    shape = (REGIONS, ELEM_REG, DOF, DOF)
    noise = jnp.clip(jax.random.normal(noise_key, shape), -4.0, 4.0)
    return dominant(centre_key, noise * (0.3 / math.sqrt(DOF)), 0.5, 1.0).astype(jnp.bfloat16)


def levels(own_key, dims, cuts, smallest, high):
    level = 1.0
    for dim, shards_of in cuts:
        heights = jax.random.uniform(jax.random.fold_in(jax.random.fold_in(own_key, 6), dim), (shards_of,), jnp.float32, smallest / len(cuts), high / len(cuts))
        level = level * jnp.repeat(jnp.exp(heights), dims[dim] // shards_of).reshape((-1,) + (1,) * (len(dims) - 1 - dim))
    return level


def gaussian(key, shape, deviation, reach, pieces=(), held_as=jnp.bfloat16):
    factor_of = levels(key, shape, pieces, -0.22, 0.18) if pieces else 1.0
    array = jax.random.normal(key, shape, jnp.float32) * deviation * factor_of
    return jnp.minimum(jnp.maximum(array, -reach), reach).astype(held_as)


def setup_inputs(seed: int = 0) -> dict:
    key_of = jax.random.split(jax.random.key(seed), 9)
    assembly_rhs = draw_assembly_rhs(jax.random.fold_in(key_of[8], 71), 0)
    source_slot = draw_source_slot(jax.random.fold_in(key_of[8], 71), 0)
    diagonal_blocks = draw_diagonal_blocks(jax.random.fold_in(key_of[8], 71), 0)
    jacobi_blocks = draw_jacobi_blocks(jax.random.fold_in(key_of[8], 71), 0)
    coupling = gaussian(key_of[4], (REGIONS, ELEM_REG, 6, FDOF, FDOF), (4 * FDOF) ** -0.5, 0.3125, ((0, 12), (1, 64)), jnp.float32)
    neighbor = draw_neighbor(jax.random.fold_in(key_of[8], 71), 0)
    neighbor_face = draw_neighbor_face(jax.random.fold_in(key_of[8], 71), 0)
    orientation = draw_orientation(jax.random.fold_in(key_of[8], 71), 0)
    return dict(assembly_rhs=assembly_rhs, source_slot=source_slot, diagonal_blocks=diagonal_blocks, jacobi_blocks=jacobi_blocks, coupling=coupling, neighbor=neighbor, neighbor_face=neighbor_face, orientation=orientation)


HIGHEST = lax.Precision.HIGHEST


def face_traces(values_in):
    lead = values_in.shape[:-1]
    shaped = values_in.reshape(lead + (NVAR, NQ, NQ, NQ))
    face_list = (shaped[..., 0, :, :], shaped[..., -1, :, :], shaped[..., :, 0, :],
                 shaped[..., :, -1, :], shaped[..., 0], shaped[..., -1])
    return jnp.stack([one_face.reshape(lead + (NVAR * NQ * NQ,)) for one_face in face_list], axis=-2)


def orient_traces(traces, orientation):
    shaped = traces.reshape(traces.shape[:-1] + (NVAR, NQ, NQ))
    flipped = shaped[..., ::-1, :].reshape(traces.shape)
    return jnp.where(orientation[..., None] == 1, flipped, traces)


def lift_faces(face_terms):
    lead = face_terms.shape[:-2]
    face_parts = face_terms.reshape(lead + (6, NVAR, NQ, NQ))
    element_cube = jnp.zeros(lead + (NVAR, NQ, NQ, NQ), face_terms.dtype)
    element_cube = element_cube.at[..., 0, :, :].add(face_parts[..., 0, :, :, :])
    element_cube = element_cube.at[..., -1, :, :].add(face_parts[..., 1, :, :, :])
    element_cube = element_cube.at[..., :, 0, :].add(face_parts[..., 2, :, :, :])
    element_cube = element_cube.at[..., :, -1, :].add(face_parts[..., 3, :, :, :])
    element_cube = element_cube.at[..., 0].add(face_parts[..., 4, :, :, :])
    element_cube = element_cube.at[..., -1].add(face_parts[..., 5, :, :, :])
    return element_cube.reshape(lead + (NVAR * NQ * NQ * NQ,))


def solve_small(gram_matrix, target):
    dimension = len(target)
    augmented = [list(gram_matrix[row_index]) + [target[row_index]] for row_index in range(dimension)]
    for pivot_row in range(dimension):
        for lower_row in range(pivot_row + 1, dimension):
            factor = augmented[lower_row][pivot_row] / augmented[pivot_row][pivot_row]
            augmented[lower_row] = [augmented[lower_row][column] - factor * augmented[pivot_row][column]
                                    for column in range(dimension + 1)]
    result = [None] * dimension
    for row_index in reversed(range(dimension)):
        value = augmented[row_index][dimension]
        for column in range(row_index + 1, dimension):
            value = value - augmented[row_index][column] * result[column]
        result[row_index] = value / augmented[row_index][row_index]
    return result


def apply_operator(values_in, diagonal_blocks, coupling, neighbor, neighbor_face, orientation):
    regions_here, elements = values_in.shape[0], values_in.shape[1]
    traces = face_traces(values_in)
    side_traces = traces[:, :, :4].reshape(regions_here, elements * 4, traces.shape[-1])
    side_rows = (neighbor * 4 + neighbor_face).reshape(-1).astype(jnp.int32)
    picked = jnp.take(side_traces, side_rows, axis=1).reshape(regions_here, elements, 4, traces.shape[-1])
    picked = orient_traces(picked, orientation)
    from_below = jnp.roll(traces[:, :, 5], 1, axis=0)
    from_above = jnp.roll(traces[:, :, 4], -1, axis=0)
    neighbor_traces = jnp.concatenate([picked, from_below[:, :, None], from_above[:, :, None]], axis=2)
    face_terms = jnp.einsum('refij,refj->refi', coupling, neighbor_traces, precision=HIGHEST)
    diagonal_part = jnp.einsum('reij,rej->rei', diagonal_blocks, values_in, precision=HIGHEST)
    return diagonal_part + lift_faces(face_terms)


def precondition(jacobi_blocks, values_in):
    def one_layer(pair):
        blocks, vector = pair
        rounded = vector.astype(jnp.bfloat16)
        return jnp.einsum('eij,ej->ei', blocks.astype(jnp.float32), rounded.astype(jnp.float32), precision=HIGHEST)
    return lax.map(one_layer, (jacobi_blocks, values_in))


def reference(assembly_rhs, source_slot, diagonal_blocks, jacobi_blocks, coupling, neighbor, neighbor_face, orientation):
    start_vec = jnp.take_along_axis(assembly_rhs, source_slot.astype(jnp.int32)[:, :, None], axis=1)
    vectors = [start_vec]
    for krylov_step in range(KRYLOV):
        vectors.append(apply_operator(precondition(jacobi_blocks, vectors[-1]), diagonal_blocks, coupling,
                                      neighbor, neighbor_face, orientation))
    gram_matrix = [[jnp.sum(vectors[1 + row_index] * vectors[1 + column]) for column in range(KRYLOV)]
                   for row_index in range(KRYLOV)]
    target = [jnp.sum(vectors[1 + row_index] * start_vec) for row_index in range(KRYLOV)]
    weights_found = solve_small(gram_matrix, target)
    combined = weights_found[0] * vectors[0]
    remaining = start_vec - weights_found[0] * vectors[1]
    for term_index in range(1, KRYLOV):
        combined = combined + weights_found[term_index] * vectors[term_index]
        remaining = remaining - weights_found[term_index] * vectors[term_index + 1]
    solution = precondition(jacobi_blocks, combined)
    return solution, remaining
```

```python
import functools

import jax
import jax.numpy as jnp
import numpy as np
from jax import lax
from jax.experimental import pallas as pl
from jax.experimental.pallas import tpu as pltpu
from jax.sharding import PartitionSpec as P

NVAR = 5
NQ = 4
DOF = NVAR * NQ**3
FDOF = NVAR * NQ**2
ELEMS = 6
PAD = 8
SLOTS = 10
PER_PAIR = 3
WIDTH = 256
WINDOW = 384
F32 = jnp.float32
BF16 = jnp.bfloat16


def face_index():
    cube = np.arange(DOF).reshape(NVAR, NQ, NQ, NQ)
    faces = (cube[:, 0], cube[:, -1], cube[:, :, 0], cube[:, :, -1], cube[..., 0], cube[..., -1])
    return np.stack([one.reshape(-1) for one in faces])


def trace_matrix():
    return (face_index()[:, :, None] == np.arange(DOF)[None, None, :]).astype(np.float32)


def params(megabytes):
    return pltpu.CompilerParams(vmem_limit_bytes=megabytes * 2**20)


def cost(flops, moved):
    return pl.CostEstimate(flops=flops, bytes_accessed=moved, transcendentals=0)


def vmem(count):
    return [pl.BlockSpec(memory_space=pltpu.VMEM)] * count


def smem():
    return pl.BlockSpec(memory_space=pltpu.SMEM)


def mul_t(rows, matrix):
    return lax.dot_general(rows, matrix, (((1,), (1,)), ((), ())), preferred_element_type=F32)


def mul(left, right):
    return lax.dot_general(left, right, (((1,), (0,)), ((), ())), preferred_element_type=F32)


def two_parts(values):
    high = values.astype(BF16)
    low = (values - high.astype(F32)).astype(BF16)
    return high, low


def stacked_parts(values):
    high = values.astype(BF16).astype(F32)
    return jnp.concatenate([high, values - high], axis=0).astype(BF16)


def own_row(result, element):
    row = lax.broadcasted_iota(jnp.int32, result[:PAD].shape, 0)
    return jnp.where(row == element, result[:PAD] + result[PAD:], 0.0)


def high_row(result, element):
    row = lax.broadcasted_iota(jnp.int32, result[:PAD].shape, 0)
    return jnp.where(row == element, result[:PAD], 0.0)


def pick_kernel(wanted_ref, rows_ref, out_ref):
    members = wanted_ref.shape[0]
    for member in range(members):
        for element in range(ELEMS):
            slot = wanted_ref[member, element]
            device = slot // SLOTS
            place = slot - device * SLOTS
            start = pl.multiple_of((place * 5 // 2) * 128, 128)
            out_ref[member, :, element * WINDOW : (element + 1) * WINDOW] = rows_ref[
                device // members, :, pl.ds(start, WINDOW)
            ]


def prepare_kernel(select_ref, jacobi_ref, coupling_ref, trace_rows_ref, high_ref, low_ref):
    for element in range(ELEMS):
        trace_rows_ref[element] = mul(select_ref[...], jacobi_ref[element]).astype(BF16)
    for block in range(6 * ELEMS):
        high, low = two_parts(coupling_ref[block])
        high_ref[block] = high
        low_ref[block] = low


def send_traces(vector, trace_rows_ref, pack_ref, send_ref, up_ref, down_ref, local_ref):
    parts = stacked_parts(vector)
    traces = []
    for face in range(6):
        rows = None
        for element in range(ELEMS):
            matrix = trace_rows_ref[element, face * FDOF : (face + 1) * FDOF, :]
            term = high_row(mul_t(parts, matrix), element)
            rows = term if rows is None else rows + term
        traces.append(rows)
    pad = jnp.zeros((PAD, 128 - FDOF), F32)
    down_ref[...] = jnp.concatenate([traces[4], pad], axis=1)
    up_ref[...] = jnp.concatenate([traces[5], pad], axis=1)
    sides = jnp.concatenate(
        [jnp.concatenate([one, jnp.zeros((PAD, WIDTH - FDOF), F32)], axis=1) for one in traces[:4]],
        axis=0,
    )
    local_ref[...] = sides[:, :128]
    spread = jnp.concatenate(
        [sides] + [pltpu.roll(sides, FDOF * place, 1) for place in range(1, PER_PAIR)], axis=0
    )
    high, low = two_parts(spread)
    send_ref[:, 0, :] = mul(pack_ref[...], high) + mul(pack_ref[...], low)


def first_kernel(
    slots_ref, rows_ref, trace_rows_ref, pack_ref,
    rhs_ref, send_ref, up_ref, down_ref, local_ref, held_ref,
):
    held_ref[...] = jnp.zeros(held_ref.shape, F32)
    for element in range(ELEMS):
        slot = slots_ref[0, element]
        device = slot // SLOTS
        place = slot - device * SLOTS
        members = rows_ref.shape[0]
        column = device - (device // members) * members
        window = rows_ref[column, :, element * WINDOW : (element + 1) * WINDOW]
        turned = pltpu.roll(window, WINDOW - 64, 1)
        odd = place - (place // 2) * 2
        held_ref[element : element + 1, :] = jnp.where(odd == 1, turned, window)
    rhs = held_ref[:, :DOF]
    rhs_ref[...] = rhs
    send_traces(rhs, trace_rows_ref, pack_ref, send_ref, up_ref, down_ref, local_ref)


def own_kernel(vector_ref, jacobi_ref, diagonal_ref, full_ref, product_ref):
    parts = stacked_parts(vector_ref[...])
    rounded = jnp.zeros((PAD, DOF), F32)
    full = jnp.zeros((PAD, DOF), F32)
    for element in range(ELEMS):
        result = mul_t(parts, jacobi_ref[element])
        rounded = rounded + high_row(result, element)
        full = full + own_row(result, element)
    full_ref[...] = full
    parts = stacked_parts(rounded)
    total = jnp.zeros((PAD, DOF), F32)
    for element in range(ELEMS):
        high, low = two_parts(diagonal_ref[element])
        total = total + own_row(mul_t(parts, high) + mul_t(parts, low), element)
    product_ref[...] = total


def add_neighbors(
    product_ref, recv_ref, below_ref, above_ref, local_ref, turn_ref,
    unpack_ref, here_ref, high_ref, low_ref, lift_ref,
):
    high, low = two_parts(recv_ref[:, 0, :])
    arrived = mul(unpack_ref[...], high) + mul(unpack_ref[...], low)
    count = 4 * PAD
    sides = arrived[:count, :128]
    for place in range(1, PER_PAIR):
        rows = arrived[place * count : (place + 1) * count]
        sides = sides + pltpu.roll(rows, WIDTH - FDOF * place, 1)[:, :128]
    high, low = two_parts(local_ref[...])
    sides = sides + mul(here_ref[...], high) + mul(here_ref[...], low)
    lane = lax.broadcasted_iota(jnp.int32, sides.shape, 1)
    step = (lane // 4) % 4
    turned = jnp.where(
        step == 0,
        pltpu.roll(sides, 128 - 12, 1),
        jnp.where(
            step == 1,
            pltpu.roll(sides, 128 - 4, 1),
            jnp.where(step == 2, pltpu.roll(sides, 4, 1), pltpu.roll(sides, 12, 1)),
        ),
    )
    sides = jnp.where(turn_ref[...] == 1, turned, sides)
    total = product_ref[...]
    for face in range(6):
        if face < 4:
            traces = sides[face * PAD : (face + 1) * PAD]
        else:
            traces = below_ref[...] if face == 4 else above_ref[...]
        parts = stacked_parts(traces[:, :FDOF])
        terms = jnp.zeros((PAD, FDOF), F32)
        for element in range(ELEMS):
            block = element * 6 + face
            terms = terms + own_row(mul_t(parts, high_ref[block]) + mul_t(parts, low_ref[block]), element)
        lifted = mul(stacked_parts(terms), lift_ref[face])
        total = total + lifted[:PAD] + lifted[PAD:]
    return total


def middle_kernel(*refs):
    operand, (trace_rows_ref, pack_ref), outs = refs[:11], refs[11:13], refs[13:]
    vector_ref, send_ref, up_ref, down_ref, local_ref = outs
    vector = add_neighbors(*operand)
    vector_ref[...] = vector
    send_traces(vector, trace_rows_ref, pack_ref, send_ref, up_ref, down_ref, local_ref)


def last_kernel(*refs):
    operand, (rhs_ref, first_ref, vector_ref, sums_ref) = refs[:11], refs[11:]
    second = add_neighbors(*operand)
    vector_ref[...] = second
    first, rhs = first_ref[...], rhs_ref[...]
    lane = lax.broadcasted_iota(jnp.int32, (1, 128), 1)
    sums = jnp.zeros((1, 128), F32)
    pairs = ((first, first), (first, second), (second, second), (first, rhs), (second, rhs))
    for place, (one, other) in enumerate(pairs):
        sums = jnp.where(lane == place, jnp.sum(one * other), sums)
    for copy in range(sums_ref.shape[0]):
        sums_ref[copy] = sums


def spread_kernel(parts_ref, sums_ref):
    total = parts_ref[0]
    for part in range(1, parts_ref.shape[0]):
        total = total + parts_ref[part]
    for copy in range(sums_ref.shape[0]):
        sums_ref[copy] = total


def finish_kernel(parts_ref, rhs_ref, first_ref, second_ref, full0_ref, full1_ref, solution_ref, residual_ref):
    total = parts_ref[0]
    for part in range(1, parts_ref.shape[0]):
        total = total + parts_ref[part]
    g11, g12, g22, t1, t2 = (total[:, place : place + 1] for place in range(5))
    factor = g12 / g11
    weight2 = (t2 - factor * t1) / (g22 - factor * g12)
    weight1 = (t1 - g12 * weight2) / g11
    solution_ref[0] = (weight1 * full0_ref[...] + weight2 * full1_ref[...])[:ELEMS]
    residual_ref[0] = (rhs_ref[...] - weight1 * first_ref[...] - weight2 * second_ref[...])[:ELEMS]


def shape(*dims, dtype=F32):
    return jax.ShapeDtypeStruct(dims, dtype)


def routes(neighbor, neighbor_face, orientation, devices):
    def sides(table, fill):
        padded = jnp.pad(table.T, ((0, 0), (0, PAD - ELEMS)), constant_values=fill)
        return padded.reshape(-1)

    own = lax.axis_index("blk").astype(jnp.int32)
    near = sides(neighbor, -ELEMS)
    face = sides(neighbor_face, 0)
    turn = sides(orientation, 0)
    count = 4 * PAD
    row = jnp.arange(count, dtype=jnp.int32)
    owner = near // ELEMS
    remote = (owner != own) & (near >= 0)
    local = owner == own
    same = owner[:, None] == owner[None, :]
    own_key = row % PAD * 4 + row // PAD
    near_key = near * 4 + face
    send_place = jnp.sum(same & (own_key[None, :] < own_key[:, None]), axis=1)
    near_place = jnp.sum(same & (near_key[None, :] < near_key[:, None]), axis=1)
    device = jnp.arange(devices, dtype=jnp.int32)
    place = jnp.arange(PER_PAIR, dtype=jnp.int32)
    to = (device[:, None] == owner[None, :]) & remote[None, :]
    pack = to[:, None, :] & (place[None, :, None] == send_place[None, None, :])
    unpack = to.T[None] & (place[:, None, None] == near_place[None, :, None])
    here = local[:, None] & (row[None, :] == (face * PAD + near % ELEMS)[:, None])
    return (
        pack.reshape(devices, PER_PAIR * count).astype(BF16),
        unpack.reshape(PER_PAIR * count, devices).astype(BF16),
        here.astype(BF16),
        jnp.broadcast_to(turn[:, None], (count, 128)),
    )


def per_device(
    columns, members,
    assembly_rhs, source_slot, diagonal_blocks, jacobi_blocks, coupling, neighbor, neighbor_face, orientation,
):
    devices = columns * members
    layers = lax.axis_size("reg")
    column_groups = [[member + members * y for y in range(columns)] for member in range(members)]
    member_groups = [[member + members * y for member in range(members)] for y in range(columns)]
    select = trace_matrix()
    diagonal, jacobi = diagonal_blocks[0], jacobi_blocks[0]

    own_rows = jnp.broadcast_to(assembly_rhs.reshape(1, 1, SLOTS * DOF), (columns, 1, SLOTS * DOF))
    own_slots = jnp.broadcast_to(source_slot[:, None, :], (members, 1, ELEMS))
    wanted = lax.all_to_all(own_slots, "blk", 0, 0, axis_index_groups=member_groups, tiled=True)
    rows = lax.all_to_all(own_rows, "blk", 0, 0, axis_index_groups=column_groups, tiled=True)

    pack, unpack, here, turn = routes(neighbor, neighbor_face, orientation, devices)
    trace_rows, high, low = pl.pallas_call(
        prepare_kernel,
        out_shape=(
            shape(ELEMS, 6 * FDOF, DOF, dtype=BF16),
            shape(6 * ELEMS, FDOF, FDOF, dtype=BF16),
            shape(6 * ELEMS, FDOF, FDOF, dtype=BF16),
        ),
        in_specs=vmem(3),
        out_specs=tuple(vmem(3)),
        compiler_params=params(16),
        cost_estimate=cost(6 * 2 * 480 * 320 * 320, 6 * 2**20),
        name="prepare",
    )(jnp.asarray(select.reshape(6 * FDOF, DOF), BF16), jacobi, coupling.reshape(6 * ELEMS, FDOF, FDOF))

    picked = pl.pallas_call(
        pick_kernel,
        out_shape=shape(members, 1, ELEMS * WINDOW),
        in_specs=[smem()] + vmem(1),
        out_specs=vmem(1)[0],
        cost_estimate=cost(1000, 2**17),
        name="pick",
    )(wanted.reshape(members, ELEMS), rows)
    mine = lax.all_to_all(picked, "blk", 0, 0, axis_index_groups=member_groups, tiled=True)

    sent = (
        shape(devices, 1, WIDTH),
        shape(PAD, 128),
        shape(PAD, 128),
        shape(4 * PAD, 128),
    )
    lift = jnp.asarray(select, BF16)

    def exchange(send, up, down):
        below = lax.ppermute(up, "reg", [(i, (i + 1) % layers) for i in range(layers)])
        above = lax.ppermute(down, "reg", [((i + 1) % layers, i) for i in range(layers)])
        return lax.all_to_all(send, "blk", 0, 0, tiled=True), below, above

    def own_part(vector):
        return pl.pallas_call(
            own_kernel,
            out_shape=(shape(PAD, DOF), shape(PAD, DOF)),
            in_specs=vmem(3),
            out_specs=tuple(vmem(2)),
            compiler_params=params(16),
            cost_estimate=cost(6 * 4 * 16 * 320 * 320, 4 * 2**20),
            name="own_part",
        )(vector, jacobi, diagonal)

    rhs, send, up, down, local = pl.pallas_call(
        first_kernel,
        out_shape=(shape(PAD, DOF),) + sent,
        in_specs=[smem()] + vmem(3),
        out_specs=tuple(vmem(5)),
        scratch_shapes=[pltpu.VMEM((PAD, WINDOW), F32)],
        compiler_params=params(16),
        cost_estimate=cost(6 * 2 * 16 * 480 * 320, 2**21),
        name="first",
    )(source_slot, mine, trace_rows, pack)
    recv, below, above = exchange(send, up, down)
    full0, product = own_part(rhs)

    first, send, up, down, local1 = pl.pallas_call(
        middle_kernel,
        out_shape=(shape(PAD, DOF),) + sent,
        in_specs=vmem(13),
        out_specs=tuple(vmem(5)),
        compiler_params=params(16),
        cost_estimate=cost(6 * 4 * 16 * 480 * 320, 4 * 2**20),
        name="middle",
    )(product, recv, below, above, local, turn, unpack, here, high, low, lift, trace_rows, pack)
    recv, below, above = exchange(send, up, down)
    full1, product = own_part(first)

    second, sums = pl.pallas_call(
        last_kernel,
        out_shape=(shape(PAD, DOF), shape(layers, 1, 128)),
        in_specs=vmem(13),
        out_specs=tuple(vmem(2)),
        compiler_params=params(16),
        cost_estimate=cost(6 * 2 * 16 * 480 * 320, 2**21),
        name="last",
    )(product, recv, below, above, local1, turn, unpack, here, high, low, lift, rhs, first)
    sums = lax.all_to_all(sums, "reg", 0, 0, tiled=True)
    sums = pl.pallas_call(
        spread_kernel,
        out_shape=shape(devices, 1, 128),
        in_specs=vmem(1),
        out_specs=vmem(1)[0],
        cost_estimate=cost(2000, 2**15),
        name="spread",
    )(sums)
    sums = lax.all_to_all(sums, "blk", 0, 0, tiled=True)
    return pl.pallas_call(
        finish_kernel,
        out_shape=(shape(1, ELEMS, DOF), shape(1, ELEMS, DOF)),
        in_specs=vmem(6),
        out_specs=tuple(vmem(2)),
        cost_estimate=cost(20000, 2**16),
        name="finish",
    )(sums, rhs, first, second, full0, full1)


def solution(mesh):
    placed = (
        P("reg", "blk", None),
        P("reg", "blk"),
        P("reg", "blk", None, None),
        P("reg", "blk", None, None),
        P("reg", "blk", None, None, None),
        P("blk", None),
        P("blk", None),
        P("blk", None),
    )
    members = 8
    return jax.shard_map(
        functools.partial(per_device, mesh.shape["blk"] // members, members),
        mesh=mesh,
        in_specs=placed,
        out_specs=(P("reg", "blk", None), P("reg", "blk", None)),
        check_vma=False,
    )
```

```python
import jax
import jax.numpy as jnp
import numpy as np
from jax import lax
from jax.experimental import pallas as pl
from jax.experimental.pallas import tpu as pltpu
from jax.sharding import PartitionSpec as P

NVAR = 5
NQ = 4
DOF = NVAR * NQ**3
FDOF = NVAR * NQ**2
ELEMS = 6
PAD = 8
SLOTS = 10
PER_PAIR = 3
WIDTH = 256
F32 = jnp.float32
BF16 = jnp.bfloat16


def face_index():
    cube = np.arange(DOF).reshape(NVAR, NQ, NQ, NQ)
    faces = (cube[:, 0], cube[:, -1], cube[:, :, 0], cube[:, :, -1], cube[..., 0], cube[..., -1])
    return np.stack([one.reshape(-1) for one in faces])


def trace_matrix():
    return (face_index()[:, :, None] == np.arange(DOF)[None, None, :]).astype(np.float32)


def params(megabytes):
    return pltpu.CompilerParams(vmem_limit_bytes=megabytes * 2**20)


def cost(flops, moved):
    return pl.CostEstimate(flops=flops, bytes_accessed=moved, transcendentals=0)


def vmem(count):
    return [pl.BlockSpec(memory_space=pltpu.VMEM)] * count


def anywhere(count):
    return [pl.BlockSpec(memory_space=pl.ANY)] * count


def in_hbm(array):
    return pltpu.with_memory_space_constraint(array, pltpu.HBM)


def smem():
    return pl.BlockSpec(memory_space=pltpu.SMEM)


def mul_t(rows, matrix):
    return lax.dot_general(rows, matrix, (((1,), (1,)), ((), ())), preferred_element_type=F32)


def mul(left, right):
    return lax.dot_general(left, right, (((1,), (0,)), ((), ())), preferred_element_type=F32)


def two_parts(values):
    high = values.astype(BF16)
    low = (values - high.astype(F32)).astype(BF16)
    return high, low


def stacked_parts(values):
    high = values.astype(BF16).astype(F32)
    return jnp.concatenate([high, values - high], axis=0).astype(BF16)


def own_row(result, element):
    row = lax.broadcasted_iota(jnp.int32, result[:PAD].shape, 0)
    return jnp.where(row == element, result[:PAD] + result[PAD:], 0.0)


def high_row(result, element):
    row = lax.broadcasted_iota(jnp.int32, result[:PAD].shape, 0)
    return jnp.where(row == element, result[:PAD], 0.0)


def precondition(vector, jacobi_ref, arrive):
    parts = stacked_parts(vector)
    rounded = jnp.zeros((PAD, DOF), F32)
    full = jnp.zeros((PAD, DOF), F32)
    for element in range(ELEMS):
        arrive(element)
        result = mul_t(parts, jacobi_ref[element])
        rounded = rounded + high_row(result, element)
        full = full + own_row(result, element)
    return rounded, full


def send_traces(values, select_ref, pack_ref, send_ref, up_ref, down_ref, local_ref):
    both = mul(stacked_parts(values), select_ref[...])
    traces = both[:PAD] + both[PAD:]
    traces = [traces[:, 128 * face : 128 * (face + 1)] for face in range(6)]
    down_ref[...] = traces[4]
    up_ref[...] = traces[5]
    sides = jnp.concatenate(traces[:4], axis=0)
    local_ref[...] = sides
    sides = jnp.concatenate([sides, jnp.zeros((4 * PAD, WIDTH - 128), F32)], axis=1)
    spread = jnp.concatenate(
        [sides] + [pltpu.roll(sides, FDOF * place, 1) for place in range(1, PER_PAIR)], axis=0
    )
    high, low = two_parts(spread)
    send_ref[:, 0, :] = mul(pack_ref[...], high) + mul(pack_ref[...], low)


def repeat_kernel(rows_ref, out_ref):
    for chip in range(out_ref.shape[0] // SLOTS):
        out_ref[chip * SLOTS : (chip + 1) * SLOTS] = rows_ref[...]


def first_kernel(
    place_ref, same_ref, other_ref, jacobi_ref, select_ref, pack_ref,
    rhs_ref, values_ref, full_ref, send_ref, up_ref, down_ref, local_ref,
):
    rhs_ref[...] = jnp.zeros(rhs_ref.shape, F32)
    for element in range(ELEMS):
        place = place_ref[0, element]
        rhs_ref[element : element + 1, :] = jnp.where(
            place_ref[1, element] == 1, other_ref[place], same_ref[place]
        )
    rounded, full = precondition(rhs_ref[...], jacobi_ref, lambda element: None)
    values_ref[...] = rounded
    full_ref[...] = full
    send_traces(rounded, select_ref, pack_ref, send_ref, up_ref, down_ref, local_ref)


def fetch(source_ref, target_ref, semaphores, width):
    copies = [
        pltpu.make_async_copy(
            source_ref.at[pl.ds(element * width, width)],
            target_ref.at[pl.ds(element * width, width)],
            semaphores.at[element],
        )
        for element in range(ELEMS)
    ]
    for copy in copies:
        copy.start()
    return lambda element: copies[element].wait()


def diagonal_kernel(values_ref, diagonal_ref, product_ref, held_ref, semaphores):
    arrive = fetch(diagonal_ref, held_ref, semaphores, 1)
    parts = stacked_parts(values_ref[...])
    total = jnp.zeros((PAD, DOF), F32)
    for element in range(ELEMS):
        arrive(element)
        high, low = two_parts(held_ref[element])
        total = total + own_row(mul_t(parts, high) + mul_t(parts, low), element)
    product_ref[...] = total


def add_neighbors(
    product_ref, recv_ref, below_ref, above_ref, local_ref, turn_ref, unpack_ref, here_ref, lift_ref,
    coupling_ref, arrive,
):
    high, low = two_parts(recv_ref[:, 0, :])
    arrived = mul(unpack_ref[...], high) + mul(unpack_ref[...], low)
    count = 4 * PAD
    sides = arrived[:count, :128]
    for place in range(1, PER_PAIR):
        rows = arrived[place * count : (place + 1) * count]
        sides = sides + pltpu.roll(rows, WIDTH - FDOF * place, 1)[:, :128]
    high, low = two_parts(local_ref[...])
    sides = sides + mul(here_ref[...], high) + mul(here_ref[...], low)
    lane = lax.broadcasted_iota(jnp.int32, sides.shape, 1)
    step = (lane // 4) % 4
    turned = jnp.where(
        step == 0,
        pltpu.roll(sides, 128 - 12, 1),
        jnp.where(
            step == 1,
            pltpu.roll(sides, 128 - 4, 1),
            jnp.where(step == 2, pltpu.roll(sides, 4, 1), pltpu.roll(sides, 12, 1)),
        ),
    )
    sides = jnp.where(turn_ref[...] == 1, turned, sides)
    traces = [sides[face * PAD : (face + 1) * PAD] for face in range(4)] + [below_ref[...], above_ref[...]]
    parts = [stacked_parts(one[:, :FDOF]) for one in traces]
    terms = [jnp.zeros((PAD, FDOF), F32)] * 6
    for element in range(ELEMS):
        arrive(element)
        for face in range(6):
            high, low = two_parts(coupling_ref[element * 6 + face])
            terms[face] = terms[face] + own_row(mul_t(parts[face], high) + mul_t(parts[face], low), element)
    total = product_ref[...]
    for face in range(6):
        lifted = mul(stacked_parts(terms[face]), lift_ref[face])
        total = total + lifted[:PAD] + lifted[PAD:]
    return total


def middle_kernel(
    product_ref, recv_ref, below_ref, above_ref, local_ref, turn_ref, unpack_ref, here_ref, lift_ref,
    select_ref, pack_ref, coupling_ref, jacobi_ref,
    vector_ref, values_ref, full_ref, send_ref, up_ref, down_ref, new_local_ref,
    held_coupling_ref, held_jacobi_ref, coupling_semaphores, jacobi_semaphores,
):
    coupling_arrive = fetch(coupling_ref, held_coupling_ref, coupling_semaphores, 6)
    jacobi_arrive = fetch(jacobi_ref, held_jacobi_ref, jacobi_semaphores, 1)
    vector = add_neighbors(
        product_ref, recv_ref, below_ref, above_ref, local_ref, turn_ref, unpack_ref, here_ref, lift_ref,
        held_coupling_ref, coupling_arrive,
    )
    vector_ref[...] = vector
    rounded, full = precondition(vector, held_jacobi_ref, jacobi_arrive)
    values_ref[...] = rounded
    full_ref[...] = full
    send_traces(rounded, select_ref, pack_ref, send_ref, up_ref, down_ref, new_local_ref)


def last_kernel(
    product_ref, recv_ref, below_ref, above_ref, local_ref, turn_ref, unpack_ref, here_ref, lift_ref,
    rhs_ref, first_ref, coupling_ref,
    vector_ref, sums_ref,
    held_coupling_ref, coupling_semaphores,
):
    arrive = fetch(coupling_ref, held_coupling_ref, coupling_semaphores, 6)
    second = add_neighbors(
        product_ref, recv_ref, below_ref, above_ref, local_ref, turn_ref, unpack_ref, here_ref, lift_ref,
        held_coupling_ref, arrive,
    )
    vector_ref[...] = second
    first, rhs = first_ref[...], rhs_ref[...]
    lane = lax.broadcasted_iota(jnp.int32, (1, 128), 1)
    sums = jnp.zeros((1, 128), F32)
    pairs = ((first, first), (first, second), (second, second), (first, rhs), (second, rhs))
    for place, (one, other) in enumerate(pairs):
        sums = jnp.where(lane == place, jnp.sum(one * other), sums)
    for copy in range(sums_ref.shape[0]):
        sums_ref[copy] = sums


def spread_kernel(parts_ref, sums_ref):
    total = parts_ref[0]
    for part in range(1, parts_ref.shape[0]):
        total = total + parts_ref[part]
    for copy in range(sums_ref.shape[0]):
        sums_ref[copy] = total


def finish_kernel(parts_ref, rhs_ref, first_ref, second_ref, full0_ref, full1_ref, solution_ref, residual_ref):
    totals = [parts_ref[part] for part in range(parts_ref.shape[0])]
    while len(totals) > 1:
        totals = [one + other for one, other in zip(totals[::2], totals[1::2])] + totals[len(totals) // 2 * 2 :]
    g11, g12, g22, t1, t2 = (totals[0][:, place : place + 1] for place in range(5))
    factor = g12 / g11
    weight2 = (t2 - factor * t1) / (g22 - factor * g12)
    weight1 = (t1 - g12 * weight2) / g11
    answer = weight1 * full0_ref[...] + weight2 * full1_ref[...]
    remaining = rhs_ref[...] - weight1 * first_ref[...] - weight2 * second_ref[...]
    for element in range(ELEMS):
        solution_ref[element] = answer[element : element + 1]
        residual_ref[element] = remaining[element : element + 1]


def shape(*dims, dtype=F32):
    return jax.ShapeDtypeStruct(dims, dtype)


def routes(neighbor, neighbor_face, orientation, devices):
    def sides(table, fill):
        padded = jnp.pad(table.T, ((0, 0), (0, PAD - ELEMS)), constant_values=fill)
        return padded.reshape(-1)

    own = lax.axis_index("blk").astype(jnp.int32)
    near = sides(neighbor, -ELEMS)
    face = sides(neighbor_face, 0)
    turn = sides(orientation, 0)
    count = 4 * PAD
    row = jnp.arange(count, dtype=jnp.int32)
    owner = near // ELEMS
    remote = (owner != own) & (near >= 0)
    local = owner == own
    same = owner[:, None] == owner[None, :]
    own_key = row % PAD * 4 + row // PAD
    near_key = near * 4 + face
    send_place = jnp.sum(same & (own_key[None, :] < own_key[:, None]), axis=1)
    near_place = jnp.sum(same & (near_key[None, :] < near_key[:, None]), axis=1)
    device = jnp.arange(devices, dtype=jnp.int32)
    place = jnp.arange(PER_PAIR, dtype=jnp.int32)
    to = (device[:, None] == owner[None, :]) & remote[None, :]
    pack = to[:, None, :] & (place[None, :, None] == send_place[None, None, :])
    unpack = to.T[None] & (place[:, None, None] == near_place[None, :, None])
    here = local[:, None] & (row[None, :] == (face * PAD + near % ELEMS)[:, None])
    return (
        pack.reshape(devices, PER_PAIR * count).astype(BF16),
        unpack.reshape(PER_PAIR * count, devices).astype(BF16),
        here.astype(BF16),
        jnp.broadcast_to(turn[:, None], (count, 128)),
    )


def per_device(
    assembly_rhs, source_slot, diagonal_blocks, jacobi_blocks, coupling, neighbor, neighbor_face, orientation
):
    devices, layers = lax.axis_size("blk"), lax.axis_size("reg")
    chips = devices // 2
    select = trace_matrix()
    wide = np.zeros((6, 128, DOF), np.float32)
    wide[:, :FDOF] = select
    wide = jnp.asarray(wide.reshape(6 * 128, DOF).T, BF16)
    lift = jnp.asarray(select, BF16)
    diagonal, jacobi = diagonal_blocks[0], jacobi_blocks[0]
    coupling = coupling.reshape(6 * ELEMS, FDOF, FDOF)

    rows = jnp.transpose(assembly_rhs, (1, 0, 2))
    rows = pl.pallas_call(
        repeat_kernel,
        out_shape=shape(chips * SLOTS, 1, DOF),
        in_specs=vmem(1),
        out_specs=vmem(1)[0],
        compiler_params=params(8),
        cost_estimate=cost(1000, 2**19),
        name="repeat",
    )(rows)
    same_core = [[2 * chip + core for chip in range(chips)] for core in range(2)]
    same = lax.all_to_all(rows, "blk", 0, 0, axis_index_groups=same_core, tiled=True)
    other = lax.ppermute(same, "blk", [(device, device ^ 1) for device in range(devices)])

    owner = source_slot // SLOTS
    place = owner // 2 * SLOTS + source_slot % SLOTS
    crossed = (owner % 2 != lax.axis_index("blk") % 2).astype(jnp.int32)
    place = jnp.concatenate([place, crossed], axis=0)
    pack, unpack, here, turn = routes(neighbor, neighbor_face, orientation, devices)

    vector = shape(PAD, DOF)
    sent = (shape(devices, 1, WIDTH), shape(PAD, 128), shape(PAD, 128), shape(4 * PAD, 128))

    def exchange(send, up, down):
        below = lax.ppermute(up, "reg", [(i, (i + 1) % layers) for i in range(layers)])
        above = lax.ppermute(down, "reg", [((i + 1) % layers, i) for i in range(layers)])
        return lax.all_to_all(send, "blk", 0, 0, tiled=True), below, above

    def diagonal_part(values):
        return pl.pallas_call(
            diagonal_kernel,
            out_shape=vector,
            in_specs=vmem(1) + anywhere(1),
            out_specs=vmem(1)[0],
            scratch_shapes=[pltpu.VMEM((ELEMS, DOF, DOF), F32), pltpu.SemaphoreType.DMA((ELEMS,))],
            compiler_params=params(16),
            cost_estimate=cost(6 * 4 * 16 * 320 * 320, 4 * 2**20),
            name="diagonal_part",
        )(values, in_hbm(diagonal))

    rhs, values, full0, send, up, down, local = pl.pallas_call(
        first_kernel,
        out_shape=(vector,) * 3 + sent,
        in_specs=[smem()] + vmem(5),
        out_specs=tuple(vmem(7)),
        compiler_params=params(16),
        cost_estimate=cost(6 * 2 * 16 * 480 * 320, 2**21),
        name="first",
    )(place, same, other, jacobi, wide, pack)
    recv, below, above = exchange(send, up, down)
    product = diagonal_part(values)

    first, values, full1, send, up, down, local1 = pl.pallas_call(
        middle_kernel,
        out_shape=(vector,) * 3 + sent,
        in_specs=vmem(11) + anywhere(2),
        out_specs=tuple(vmem(7)),
        scratch_shapes=[
            pltpu.VMEM((6 * ELEMS, FDOF, FDOF), F32),
            pltpu.VMEM((ELEMS, DOF, DOF), BF16),
            pltpu.SemaphoreType.DMA((ELEMS,)),
            pltpu.SemaphoreType.DMA((ELEMS,)),
        ],
        compiler_params=params(16),
        cost_estimate=cost(6 * 4 * 16 * 480 * 320, 4 * 2**20),
        name="middle",
    )(product, recv, below, above, local, turn, unpack, here, lift, wide, pack, in_hbm(coupling), in_hbm(jacobi))
    recv, below, above = exchange(send, up, down)
    product = diagonal_part(values)

    second, sums = pl.pallas_call(
        last_kernel,
        out_shape=(vector, shape(layers, 1, 128)),
        in_specs=vmem(11) + anywhere(1),
        out_specs=tuple(vmem(2)),
        scratch_shapes=[
            pltpu.VMEM((6 * ELEMS, FDOF, FDOF), F32),
            pltpu.SemaphoreType.DMA((ELEMS,)),
        ],
        compiler_params=params(16),
        cost_estimate=cost(6 * 2 * 16 * 480 * 320, 2**21),
        name="last",
    )(product, recv, below, above, local1, turn, unpack, here, lift, rhs, first, in_hbm(coupling))
    sums = lax.all_to_all(sums, "reg", 0, 0, tiled=True)
    sums = pl.pallas_call(
        spread_kernel,
        out_shape=shape(devices, 1, 128),
        in_specs=vmem(1),
        out_specs=vmem(1)[0],
        compiler_params=params(8),
        cost_estimate=cost(2000, 2**15),
        name="spread",
    )(sums)
    sums = lax.all_to_all(sums, "blk", 0, 0, tiled=True)
    answer, remaining = pl.pallas_call(
        finish_kernel,
        out_shape=(shape(ELEMS, 1, DOF), shape(ELEMS, 1, DOF)),
        in_specs=vmem(6),
        out_specs=tuple(vmem(2)),
        compiler_params=params(8),
        cost_estimate=cost(20000, 2**16),
        name="finish",
    )(sums, rhs, first, second, full0, full1)
    return jnp.transpose(answer, (1, 0, 2)), jnp.transpose(remaining, (1, 0, 2))


def solution(mesh):
    placed = (
        P("reg", "blk", None),
        P("reg", "blk"),
        P("reg", "blk", None, None),
        P("reg", "blk", None, None),
        P("reg", "blk", None, None, None),
        P("blk", None),
        P("blk", None),
        P("blk", None),
    )
    return jax.shard_map(
        per_device,
        mesh=mesh,
        in_specs=placed,
        out_specs=(P("reg", "blk", None), P("reg", "blk", None)),
        check_vma=False,
    )
```

```python
import jax
import jax.numpy as jnp
import numpy as np
from jax import lax
from jax.experimental import pallas as pl
from jax.experimental.pallas import tpu as pltpu
from jax.sharding import PartitionSpec as P

NVAR = 5
NQ = 4
DOF = NVAR * NQ**3
FDOF = NVAR * NQ**2
ELEMS = 6
PAD = 8
SLOTS = 10
WINDOW = 384
PER_PAIR = 3
WIDTH = 256
F32 = jnp.float32
BF16 = jnp.bfloat16


def face_index():
    cube = np.arange(DOF).reshape(NVAR, NQ, NQ, NQ)
    faces = (cube[:, 0], cube[:, -1], cube[:, :, 0], cube[:, :, -1], cube[..., 0], cube[..., -1])
    return np.stack([one.reshape(-1) for one in faces])


def trace_matrix():
    return (face_index()[:, :, None] == np.arange(DOF)[None, None, :]).astype(np.float32)


def params(megabytes):
    return pltpu.CompilerParams(vmem_limit_bytes=megabytes * 2**20)


def cost(flops, moved):
    return pl.CostEstimate(flops=flops, bytes_accessed=moved, transcendentals=0)


def vmem(count):
    return [pl.BlockSpec(memory_space=pltpu.VMEM)] * count


def anywhere(count):
    return [pl.BlockSpec(memory_space=pl.ANY)] * count


def in_hbm(array):
    return pltpu.with_memory_space_constraint(array, pltpu.HBM)


def smem():
    return pl.BlockSpec(memory_space=pltpu.SMEM)


def mul_t(rows, matrix):
    return lax.dot_general(rows, matrix, (((1,), (1,)), ((), ())), preferred_element_type=F32)


def mul(left, right):
    return lax.dot_general(left, right, (((1,), (0,)), ((), ())), preferred_element_type=F32)


def two_parts(values):
    high = values.astype(BF16)
    low = (values - high.astype(F32)).astype(BF16)
    return high, low


def stacked_parts(values):
    high = values.astype(BF16).astype(F32)
    return jnp.concatenate([high, values - high], axis=0).astype(BF16)


def own_row(result, element):
    row = lax.broadcasted_iota(jnp.int32, result[:PAD].shape, 0)
    return jnp.where(row == element, result[:PAD] + result[PAD:], 0.0)


def high_row(result, element):
    row = lax.broadcasted_iota(jnp.int32, result[:PAD].shape, 0)
    return jnp.where(row == element, result[:PAD], 0.0)


def precondition(vector, jacobi_ref):
    parts = stacked_parts(vector)
    rounded = jnp.zeros((PAD, DOF), F32)
    full = jnp.zeros((PAD, DOF), F32)
    for element in range(ELEMS):
        result = mul_t(parts, jacobi_ref[element])
        rounded = rounded + high_row(result, element)
        full = full + own_row(result, element)
    return rounded, full


def send_traces(values, select_ref, pack_ref, send_ref, up_ref, down_ref, local_ref):
    both = mul_t(stacked_parts(values), select_ref[...])
    traces = both[:PAD] + both[PAD:]
    pad = jnp.zeros((PAD, 128 - FDOF), F32)
    traces = [
        jnp.concatenate([traces[:, FDOF * face : FDOF * (face + 1)], pad], axis=1) for face in range(6)
    ]
    down_ref[...] = traces[4]
    up_ref[...] = traces[5]
    sides = jnp.concatenate(traces[:4], axis=0)
    local_ref[...] = sides
    sides = jnp.concatenate([sides, jnp.zeros((4 * PAD, WIDTH - 128), F32)], axis=1)
    spread = jnp.concatenate(
        [sides] + [pltpu.roll(sides, FDOF * place, 1) for place in range(1, PER_PAIR)], axis=0
    )
    high, low = two_parts(spread)
    send_ref[:, 0, :] = mul(pack_ref[...], high) + mul(pack_ref[...], low)


def repeat_kernel(rows_ref, out_ref):
    flat = jnp.concatenate([rows_ref[slot] for slot in range(SLOTS)], axis=1)
    for chip in range(out_ref.shape[0]):
        out_ref[chip] = flat


def hold_kernel(far_ref, near_ref):
    near_ref[...] = far_ref[...]


def first_kernel(
    place_ref, same_ref, other_ref, jacobi_ref, pack_ref, select_ref,
    rhs_ref, values_ref, full_ref, send_ref, up_ref, down_ref, local_ref, held_ref,
):
    held_ref[...] = jnp.zeros(held_ref.shape, F32)
    for element in range(ELEMS):
        chip, slot = place_ref[0, element], place_ref[1, element]
        lanes = pl.ds(pl.multiple_of((slot * 5 // 2) * 128, 128), WINDOW)
        window = jnp.where(place_ref[2, element] == 1, other_ref[chip, :, lanes], same_ref[chip, :, lanes])
        turned = pltpu.roll(window, WINDOW - 64, 1)
        held_ref[element : element + 1, :] = jnp.where(slot % 2 == 1, turned, window)
    rhs_ref[...] = held_ref[:, :DOF]
    rounded, full = precondition(rhs_ref[...], jacobi_ref)
    values_ref[...] = rounded
    full_ref[...] = full
    send_traces(rounded, select_ref, pack_ref, send_ref, up_ref, down_ref, local_ref)


def fetch(source_ref, target_ref, semaphores):
    copies = [
        pltpu.make_async_copy(source_ref.at[element], target_ref.at[element], semaphores.at[element])
        for element in range(ELEMS)
    ]
    for copy in copies:
        copy.start()
    return lambda element: copies[element].wait()


def diagonal_kernel(values_ref, diagonal_ref, product_ref, held_ref, semaphores):
    arrive = fetch(diagonal_ref, held_ref, semaphores)
    parts = stacked_parts(values_ref[...])
    total = jnp.zeros((PAD, DOF), F32)
    for element in range(ELEMS):
        arrive(element)
        high, low = two_parts(held_ref[element])
        total = total + own_row(mul_t(parts, high) + mul_t(parts, low), element)
    product_ref[...] = total


def add_neighbors(
    product_ref, recv_ref, below_ref, above_ref, local_ref, turn_ref, unpack_ref, here_ref, coupling_ref,
    select_ref, copy,
):
    high, low = two_parts(recv_ref[:, 0, :])
    arrived = mul(unpack_ref[...], high) + mul(unpack_ref[...], low)
    count = 4 * PAD
    sides = arrived[:count, :128]
    for place in range(1, PER_PAIR):
        rows = arrived[place * count : (place + 1) * count]
        sides = sides + pltpu.roll(rows, WIDTH - FDOF * place, 1)[:, :128]
    high, low = two_parts(local_ref[...])
    sides = sides + mul(here_ref[...], high) + mul(here_ref[...], low)
    lane = lax.broadcasted_iota(jnp.int32, sides.shape, 1)
    step = (lane // 4) % 4
    turned = jnp.where(
        step == 0,
        pltpu.roll(sides, 128 - 12, 1),
        jnp.where(
            step == 1,
            pltpu.roll(sides, 128 - 4, 1),
            jnp.where(step == 2, pltpu.roll(sides, 4, 1), pltpu.roll(sides, 12, 1)),
        ),
    )
    sides = jnp.where(turn_ref[...] == 1, turned, sides)
    traces = [sides[face * PAD : (face + 1) * PAD] for face in range(4)] + [below_ref[...], above_ref[...]]
    parts = [stacked_parts(one[:, :FDOF]) for one in traces]
    terms = [jnp.zeros((PAD, FDOF), F32)] * 6
    for face in range(6):
        blocks = jnp.concatenate([coupling_ref[element * 6 + face] for element in range(ELEMS)], axis=0)
        high, low = two_parts(blocks)
        result = mul_t(parts[face], high) + mul_t(parts[face], low)
        for element in range(ELEMS):
            own = result[:, element * FDOF : (element + 1) * FDOF]
            terms[face] = terms[face] + own_row(own, element)
    copy.wait()
    total = product_ref[...]
    for face in range(6):
        lifted = mul(stacked_parts(terms[face]), select_ref[face * FDOF : (face + 1) * FDOF, :])
        total = total + lifted[:PAD] + lifted[PAD:]
    return total


def middle_kernel(
    product_ref, recv_ref, below_ref, above_ref, local_ref, turn_ref, unpack_ref, here_ref, coupling_ref,
    pack_ref, jacobi_ref, far_select_ref,
    vector_ref, values_ref, full_ref, send_ref, up_ref, down_ref, new_local_ref,
    select_ref, semaphore,
):
    copy = pltpu.make_async_copy(far_select_ref, select_ref, semaphore)
    copy.start()
    vector = add_neighbors(
        product_ref, recv_ref, below_ref, above_ref, local_ref, turn_ref, unpack_ref, here_ref, coupling_ref,
        select_ref, copy,
    )
    vector_ref[...] = vector
    rounded, full = precondition(vector, jacobi_ref)
    values_ref[...] = rounded
    full_ref[...] = full
    send_traces(rounded, select_ref, pack_ref, send_ref, up_ref, down_ref, new_local_ref)


def last_kernel(
    product_ref, recv_ref, below_ref, above_ref, local_ref, turn_ref, unpack_ref, here_ref, coupling_ref,
    rhs_ref, first_ref, far_select_ref,
    vector_ref, sums_ref,
    select_ref, semaphore,
):
    copy = pltpu.make_async_copy(far_select_ref, select_ref, semaphore)
    copy.start()
    second = add_neighbors(
        product_ref, recv_ref, below_ref, above_ref, local_ref, turn_ref, unpack_ref, here_ref, coupling_ref,
        select_ref, copy,
    )
    vector_ref[...] = second
    first, rhs = first_ref[...], rhs_ref[...]
    lane = lax.broadcasted_iota(jnp.int32, (1, 128), 1)
    sums = jnp.zeros((1, 128), F32)
    pairs = ((first, first), (first, second), (second, second), (first, rhs), (second, rhs))
    for place, (one, other) in enumerate(pairs):
        sums = jnp.where(lane == place, jnp.sum(one * other), sums)
    for copy in range(sums_ref.shape[0]):
        sums_ref[copy] = sums


def spread_kernel(parts_ref, sums_ref):
    total = parts_ref[0]
    for part in range(1, parts_ref.shape[0]):
        total = total + parts_ref[part]
    for copy in range(sums_ref.shape[0]):
        sums_ref[copy] = total


def finish_kernel(parts_ref, rhs_ref, first_ref, second_ref, full0_ref, full1_ref, solution_ref, residual_ref):
    totals = [parts_ref[part] for part in range(parts_ref.shape[0])]
    while len(totals) > 1:
        totals = [one + other for one, other in zip(totals[::2], totals[1::2])] + totals[len(totals) // 2 * 2 :]
    g11, g12, g22, t1, t2 = (totals[0][:, place : place + 1] for place in range(5))
    factor = g12 / g11
    weight2 = (t2 - factor * t1) / (g22 - factor * g12)
    weight1 = (t1 - g12 * weight2) / g11
    answer = weight1 * full0_ref[...] + weight2 * full1_ref[...]
    remaining = rhs_ref[...] - weight1 * first_ref[...] - weight2 * second_ref[...]
    for element in range(ELEMS):
        solution_ref[element] = answer[element : element + 1]
        residual_ref[element] = remaining[element : element + 1]


def shape(*dims, dtype=F32):
    return jax.ShapeDtypeStruct(dims, dtype)


def routes(neighbor, neighbor_face, orientation, devices):
    def sides(table, fill):
        padded = jnp.pad(table.T, ((0, 0), (0, PAD - ELEMS)), constant_values=fill)
        return padded.reshape(-1)

    own = lax.axis_index("blk").astype(jnp.int32)
    near = sides(neighbor, -ELEMS)
    face = sides(neighbor_face, 0)
    turn = sides(orientation, 0)
    count = 4 * PAD
    row = jnp.arange(count, dtype=jnp.int32)
    owner = near // ELEMS
    remote = (owner != own) & (near >= 0)
    local = owner == own
    same = owner[:, None] == owner[None, :]
    own_key = row % PAD * 4 + row // PAD
    near_key = near * 4 + face
    send_place = jnp.sum(same & (own_key[None, :] < own_key[:, None]), axis=1)
    near_place = jnp.sum(same & (near_key[None, :] < near_key[:, None]), axis=1)
    device = jnp.arange(devices, dtype=jnp.int32)
    place = jnp.arange(PER_PAIR, dtype=jnp.int32)
    to = (device[:, None] == owner[None, :]) & remote[None, :]
    pack = to[:, None, :] & (place[None, :, None] == send_place[None, None, :])
    unpack = to.T[None] & (place[:, None, None] == near_place[None, :, None])
    here = local[:, None] & (row[None, :] == (face * PAD + near % ELEMS)[:, None])
    return (
        pack.reshape(devices, PER_PAIR * count).astype(BF16),
        unpack.reshape(PER_PAIR * count, devices).astype(BF16),
        here.astype(BF16),
        jnp.broadcast_to(turn[:, None], (count, 128)),
    )


def per_device(
    assembly_rhs, source_slot, diagonal_blocks, jacobi_blocks, coupling, neighbor, neighbor_face, orientation
):
    devices, layers = lax.axis_size("blk"), lax.axis_size("reg")
    chips = devices // 2
    select = jnp.asarray(trace_matrix().reshape(6 * FDOF, DOF), BF16)
    near_select = pl.pallas_call(
        hold_kernel,
        out_shape=shape(6 * FDOF, DOF, dtype=BF16),
        in_specs=vmem(1),
        out_specs=vmem(1)[0],
        compiler_params=params(8),
        cost_estimate=cost(100000, 2**20),
        name="hold",
    )(select)
    select = in_hbm(select)
    held_select = [pltpu.VMEM((6 * FDOF, DOF), BF16), pltpu.SemaphoreType.DMA]
    diagonal, jacobi = diagonal_blocks[0], jacobi_blocks[0]
    coupling = coupling.reshape(6 * ELEMS, FDOF, FDOF)

    rows = jnp.transpose(assembly_rhs, (1, 0, 2))
    rows = pl.pallas_call(
        repeat_kernel,
        out_shape=shape(chips, 1, SLOTS * DOF),
        in_specs=vmem(1),
        out_specs=vmem(1)[0],
        compiler_params=params(8),
        cost_estimate=cost(1000, 2**19),
        name="repeat",
    )(rows)
    same_core = [[2 * chip + core for chip in range(chips)] for core in range(2)]
    same = lax.all_to_all(rows, "blk", 0, 0, axis_index_groups=same_core, tiled=True)
    other = lax.ppermute(same, "blk", [(device, device ^ 1) for device in range(devices)])

    owner = source_slot // SLOTS
    crossed = (owner % 2 != lax.axis_index("blk") % 2).astype(jnp.int32)
    place = jnp.concatenate([owner // 2, source_slot % SLOTS, crossed], axis=0)
    pack, unpack, here, turn = routes(neighbor, neighbor_face, orientation, devices)

    vector = shape(PAD, DOF)
    sent = (shape(devices, 1, WIDTH), shape(PAD, 128), shape(PAD, 128), shape(4 * PAD, 128))

    def exchange(send, up, down):
        below = lax.ppermute(up, "reg", [(i, (i + 1) % layers) for i in range(layers)])
        above = lax.ppermute(down, "reg", [((i + 1) % layers, i) for i in range(layers)])
        return lax.all_to_all(send, "blk", 0, 0, tiled=True), below, above

    def diagonal_part(values):
        return pl.pallas_call(
            diagonal_kernel,
            out_shape=vector,
            in_specs=vmem(1) + anywhere(1),
            out_specs=vmem(1)[0],
            scratch_shapes=[pltpu.VMEM((ELEMS, DOF, DOF), F32), pltpu.SemaphoreType.DMA((ELEMS,))],
            compiler_params=params(16),
            cost_estimate=cost(6 * 4 * 16 * 320 * 320, 4 * 2**20),
            name="diagonal_part",
        )(values, in_hbm(diagonal))

    rhs, values, full0, send, up, down, local = pl.pallas_call(
        first_kernel,
        out_shape=(vector,) * 3 + sent,
        in_specs=[smem()] + vmem(5),
        scratch_shapes=[pltpu.VMEM((PAD, WINDOW), F32)],
        out_specs=tuple(vmem(7)),
        compiler_params=params(16),
        cost_estimate=cost(6 * 2 * 16 * 480 * 320, 2**21),
        name="first",
    )(place, same, other, jacobi, pack, near_select)
    recv, below, above = exchange(send, up, down)
    product = diagonal_part(values)

    first, values, full1, send, up, down, local1 = pl.pallas_call(
        middle_kernel,
        out_shape=(vector,) * 3 + sent,
        in_specs=vmem(11) + anywhere(1),
        scratch_shapes=held_select,
        out_specs=tuple(vmem(7)),
        compiler_params=params(16),
        cost_estimate=cost(6 * 4 * 16 * 480 * 320, 4 * 2**20),
        name="middle",
    )(product, recv, below, above, local, turn, unpack, here, coupling, pack, jacobi, select)
    recv, below, above = exchange(send, up, down)
    product = diagonal_part(values)

    second, sums = pl.pallas_call(
        last_kernel,
        out_shape=(vector, shape(layers, 1, 128)),
        in_specs=vmem(11) + anywhere(1),
        scratch_shapes=held_select,
        out_specs=tuple(vmem(2)),
        compiler_params=params(16),
        cost_estimate=cost(6 * 2 * 16 * 480 * 320, 2**21),
        name="last",
    )(product, recv, below, above, local1, turn, unpack, here, coupling, rhs, first, select)
    sums = lax.all_to_all(sums, "reg", 0, 0, tiled=True)
    sums = pl.pallas_call(
        spread_kernel,
        out_shape=shape(devices, 1, 128),
        in_specs=vmem(1),
        out_specs=vmem(1)[0],
        compiler_params=params(8),
        cost_estimate=cost(2000, 2**15),
        name="spread",
    )(sums)
    sums = lax.all_to_all(sums, "blk", 0, 0, tiled=True)
    answer, remaining = pl.pallas_call(
        finish_kernel,
        out_shape=(shape(ELEMS, 1, DOF), shape(ELEMS, 1, DOF)),
        in_specs=vmem(6),
        out_specs=tuple(vmem(2)),
        compiler_params=params(8),
        cost_estimate=cost(20000, 2**16),
        name="finish",
    )(sums, rhs, first, second, full0, full1)
    return jnp.transpose(answer, (1, 0, 2)), jnp.transpose(remaining, (1, 0, 2))


def solution(mesh):
    placed = (
        P("reg", "blk", None),
        P("reg", "blk"),
        P("reg", "blk", None, None),
        P("reg", "blk", None, None),
        P("reg", "blk", None, None, None),
        P("blk", None),
        P("blk", None),
        P("blk", None),
    )
    return jax.shard_map(
        per_device,
        mesh=mesh,
        in_specs=placed,
        out_specs=(P("reg", "blk", None), P("reg", "blk", None)),
        check_vma=False,
    )
```

```python
import jax
import jax.numpy as jnp
from jax import lax
from jax.experimental import pallas as pl
from jax.experimental.pallas import tpu as pltpu
from jax.sharding import PartitionSpec as P

NVAR = 5
NQ = 4
DOF = NVAR * NQ**3
FDOF = NVAR * NQ**2
ELEMS = 6
PAD = 8
SLOTS = 10
WINDOW = 384
PER_PAIR = 3
WIDTH = 256
F32 = jnp.float32
BF16 = jnp.bfloat16


def fill_select(select_ref):
    row = lax.broadcasted_iota(jnp.int32, (FDOF, DOF), 0)
    entry = lax.broadcasted_iota(jnp.int32, (FDOF, DOF), 1)
    variable = (row >> 4) << 6
    first, second = (row >> 2) & 3, row & 3
    along_i = variable + (row & 15)
    along_j = variable + (first << 4) + second
    along_k = variable + ((row & 15) << 2)
    last = NQ - 1
    places = (along_i, along_i + 16 * last, along_j, along_j + 4 * last, along_k, along_k + last)
    for face, place in enumerate(places):
        select_ref[face * FDOF : (face + 1) * FDOF, :] = jnp.where(entry == place, 1.0, 0.0).astype(BF16)


def params(megabytes):
    return pltpu.CompilerParams(vmem_limit_bytes=megabytes * 2**20)


def cost(flops, moved):
    return pl.CostEstimate(flops=flops, bytes_accessed=moved, transcendentals=0)


def vmem(count):
    return [pl.BlockSpec(memory_space=pltpu.VMEM)] * count


def anywhere(count):
    return [pl.BlockSpec(memory_space=pl.ANY)] * count


def in_hbm(array):
    return pltpu.with_memory_space_constraint(array, pltpu.HBM)


def smem():
    return pl.BlockSpec(memory_space=pltpu.SMEM)


def mul_t(rows, matrix):
    return lax.dot_general(rows, matrix, (((1,), (1,)), ((), ())), preferred_element_type=F32)


def mul(left, right):
    return lax.dot_general(left, right, (((1,), (0,)), ((), ())), preferred_element_type=F32)


def two_parts(values):
    high = values.astype(BF16)
    low = (values - high.astype(F32)).astype(BF16)
    return high, low


def stacked_parts(values):
    high = values.astype(BF16).astype(F32)
    return jnp.concatenate([high, values - high], axis=0).astype(BF16)


def own_row(result, element):
    row = lax.broadcasted_iota(jnp.int32, result[:PAD].shape, 0)
    return jnp.where(row == element, result[:PAD] + result[PAD:], 0.0)


def high_row(result, element):
    row = lax.broadcasted_iota(jnp.int32, result[:PAD].shape, 0)
    return jnp.where(row == element, result[:PAD], 0.0)


def precondition(vector, jacobi_ref):
    parts = stacked_parts(vector)
    rounded = jnp.zeros((PAD, DOF), F32)
    full = jnp.zeros((PAD, DOF), F32)
    for element in range(ELEMS):
        result = mul_t(parts, jacobi_ref[element])
        rounded = rounded + high_row(result, element)
        full = full + own_row(result, element)
    return rounded, full


def send_traces(values, select_ref, pack_ref, send_ref, up_ref, down_ref, local_ref):
    both = mul_t(stacked_parts(values), select_ref[...])
    traces = both[:PAD] + both[PAD:]
    pad = jnp.zeros((PAD, 128 - FDOF), F32)
    traces = [
        jnp.concatenate([traces[:, FDOF * face : FDOF * (face + 1)], pad], axis=1) for face in range(6)
    ]
    down_ref[...] = traces[4]
    up_ref[...] = traces[5]
    sides = jnp.concatenate(traces[:4], axis=0)
    local_ref[...] = sides
    sides = jnp.concatenate([sides, jnp.zeros((4 * PAD, WIDTH - 128), F32)], axis=1)
    spread = jnp.concatenate(
        [sides] + [pltpu.roll(sides, FDOF * place, 1) for place in range(1, PER_PAIR)], axis=0
    )
    high, low = two_parts(spread)
    send_ref[:, 0, :] = mul(pack_ref[...], high) + mul(pack_ref[...], low)


def repeat_kernel(rows_ref, out_ref):
    flat = jnp.concatenate([rows_ref[slot] for slot in range(SLOTS)], axis=1)
    for chip in range(out_ref.shape[0]):
        out_ref[chip] = flat


def hold_kernel(far_ref, near_ref, semaphore):
    copy = pltpu.make_async_copy(far_ref, near_ref, semaphore)
    copy.start()
    copy.wait()


def first_kernel(
    place_ref, same_ref, other_ref, jacobi_ref, pack_ref,
    rhs_ref, values_ref, full_ref, send_ref, up_ref, down_ref, local_ref,
    select_ref, held_ref,
):
    fill_select(select_ref)
    held_ref[...] = jnp.zeros(held_ref.shape, F32)
    for element in range(ELEMS):
        chip, slot = place_ref[0, element], place_ref[1, element]
        lanes = pl.ds(pl.multiple_of((slot * 5 // 2) * 128, 128), WINDOW)
        window = jnp.where(place_ref[2, element] == 1, other_ref[chip, :, lanes], same_ref[chip, :, lanes])
        turned = pltpu.roll(window, WINDOW - 64, 1)
        held_ref[element : element + 1, :] = jnp.where(slot % 2 == 1, turned, window)
    rhs_ref[...] = held_ref[:, :DOF]
    rounded, full = precondition(rhs_ref[...], jacobi_ref)
    values_ref[...] = rounded
    full_ref[...] = full
    send_traces(rounded, select_ref, pack_ref, send_ref, up_ref, down_ref, local_ref)


def fetch(source_ref, target_ref, semaphores):
    copies = [
        pltpu.make_async_copy(source_ref.at[element], target_ref.at[element], semaphores.at[element])
        for element in range(ELEMS)
    ]
    for copy in copies:
        copy.start()
    return lambda element: copies[element].wait()


def diagonal_kernel(values_ref, diagonal_ref, product_ref, held_ref, semaphores):
    arrive = fetch(diagonal_ref, held_ref, semaphores)
    parts = stacked_parts(values_ref[...])
    total = jnp.zeros((PAD, DOF), F32)
    for element in range(ELEMS):
        arrive(element)
        high, low = two_parts(held_ref[element])
        total = total + own_row(mul_t(parts, high) + mul_t(parts, low), element)
    product_ref[...] = total


def add_neighbors(
    product_ref, recv_ref, below_ref, above_ref, local_ref, turn_ref, unpack_ref, here_ref, coupling_ref,
    select_ref,
):
    high, low = two_parts(recv_ref[:, 0, :])
    arrived = mul(unpack_ref[...], high) + mul(unpack_ref[...], low)
    count = 4 * PAD
    sides = arrived[:count, :128]
    for place in range(1, PER_PAIR):
        rows = arrived[place * count : (place + 1) * count]
        sides = sides + pltpu.roll(rows, WIDTH - FDOF * place, 1)[:, :128]
    high, low = two_parts(local_ref[...])
    sides = sides + mul(here_ref[...], high) + mul(here_ref[...], low)
    lane = lax.broadcasted_iota(jnp.int32, sides.shape, 1)
    step = (lane // 4) % 4
    turned = jnp.where(
        step == 0,
        pltpu.roll(sides, 128 - 12, 1),
        jnp.where(
            step == 1,
            pltpu.roll(sides, 128 - 4, 1),
            jnp.where(step == 2, pltpu.roll(sides, 4, 1), pltpu.roll(sides, 12, 1)),
        ),
    )
    sides = jnp.where(turn_ref[...] == 1, turned, sides)
    traces = [sides[face * PAD : (face + 1) * PAD] for face in range(4)] + [below_ref[...], above_ref[...]]
    parts = [stacked_parts(one[:, :FDOF]) for one in traces]
    terms = [jnp.zeros((PAD, FDOF), F32)] * 6
    for face in range(6):
        blocks = jnp.concatenate([coupling_ref[element * 6 + face] for element in range(ELEMS)], axis=0)
        high, low = two_parts(blocks)
        result = mul_t(parts[face], high) + mul_t(parts[face], low)
        for element in range(ELEMS):
            own = result[:, element * FDOF : (element + 1) * FDOF]
            terms[face] = terms[face] + own_row(own, element)
    total = product_ref[...]
    for face in range(6):
        lifted = mul(stacked_parts(terms[face]), select_ref[face * FDOF : (face + 1) * FDOF, :])
        total = total + lifted[:PAD] + lifted[PAD:]
    return total


def middle_kernel(
    product_ref, recv_ref, below_ref, above_ref, local_ref, turn_ref, unpack_ref, here_ref, coupling_ref,
    pack_ref, jacobi_ref,
    vector_ref, values_ref, full_ref, send_ref, up_ref, down_ref, new_local_ref,
    select_ref,
):
    fill_select(select_ref)
    vector = add_neighbors(
        product_ref, recv_ref, below_ref, above_ref, local_ref, turn_ref, unpack_ref, here_ref, coupling_ref,
        select_ref,
    )
    vector_ref[...] = vector
    rounded, full = precondition(vector, jacobi_ref)
    values_ref[...] = rounded
    full_ref[...] = full
    send_traces(rounded, select_ref, pack_ref, send_ref, up_ref, down_ref, new_local_ref)


def last_kernel(
    product_ref, recv_ref, below_ref, above_ref, local_ref, turn_ref, unpack_ref, here_ref, coupling_ref,
    rhs_ref, first_ref,
    vector_ref, sums_ref,
    select_ref,
):
    fill_select(select_ref)
    second = add_neighbors(
        product_ref, recv_ref, below_ref, above_ref, local_ref, turn_ref, unpack_ref, here_ref, coupling_ref,
        select_ref,
    )
    vector_ref[...] = second
    first, rhs = first_ref[...], rhs_ref[...]
    lane = lax.broadcasted_iota(jnp.int32, (1, 128), 1)
    sums = jnp.zeros((1, 128), F32)
    pairs = ((first, first), (first, second), (second, second), (first, rhs), (second, rhs))
    for place, (one, other) in enumerate(pairs):
        sums = jnp.where(lane == place, jnp.sum(one * other), sums)
    for copy in range(sums_ref.shape[0]):
        sums_ref[copy] = sums


def spread_kernel(parts_ref, sums_ref):
    total = parts_ref[0]
    for part in range(1, parts_ref.shape[0]):
        total = total + parts_ref[part]
    for copy in range(sums_ref.shape[0]):
        sums_ref[copy] = total


def finish_kernel(parts_ref, rhs_ref, first_ref, second_ref, full0_ref, full1_ref, solution_ref, residual_ref):
    totals = [parts_ref[part] for part in range(parts_ref.shape[0])]
    while len(totals) > 1:
        totals = [one + other for one, other in zip(totals[::2], totals[1::2])] + totals[len(totals) // 2 * 2 :]
    g11, g12, g22, t1, t2 = (totals[0][:, place : place + 1] for place in range(5))
    factor = g12 / g11
    weight2 = (t2 - factor * t1) / (g22 - factor * g12)
    weight1 = (t1 - g12 * weight2) / g11
    answer = weight1 * full0_ref[...] + weight2 * full1_ref[...]
    remaining = rhs_ref[...] - weight1 * first_ref[...] - weight2 * second_ref[...]
    for element in range(ELEMS):
        solution_ref[element] = answer[element : element + 1]
        residual_ref[element] = remaining[element : element + 1]


def shape(*dims, dtype=F32):
    return jax.ShapeDtypeStruct(dims, dtype)


def routes(neighbor, neighbor_face, orientation, devices):
    def sides(table, fill):
        padded = jnp.pad(table.T, ((0, 0), (0, PAD - ELEMS)), constant_values=fill)
        return padded.reshape(-1)

    own = lax.axis_index("blk").astype(jnp.int32)
    near = sides(neighbor, -ELEMS)
    face = sides(neighbor_face, 0)
    turn = sides(orientation, 0)
    count = 4 * PAD
    row = jnp.arange(count, dtype=jnp.int32)
    owner = near // ELEMS
    remote = (owner != own) & (near >= 0)
    local = owner == own
    same = owner[:, None] == owner[None, :]
    own_key = row % PAD * 4 + row // PAD
    near_key = near * 4 + face
    send_place = jnp.sum(same & (own_key[None, :] < own_key[:, None]), axis=1)
    near_place = jnp.sum(same & (near_key[None, :] < near_key[:, None]), axis=1)
    device = jnp.arange(devices, dtype=jnp.int32)
    place = jnp.arange(PER_PAIR, dtype=jnp.int32)
    to = (device[:, None] == owner[None, :]) & remote[None, :]
    pack = to[:, None, :] & (place[None, :, None] == send_place[None, None, :])
    unpack = to.T[None] & (place[:, None, None] == near_place[None, :, None])
    here = local[:, None] & (row[None, :] == (face * PAD + near % ELEMS)[:, None])
    return (
        pack.reshape(devices, PER_PAIR * count).astype(BF16),
        unpack.reshape(PER_PAIR * count, devices).astype(BF16),
        here.astype(BF16),
        jnp.broadcast_to(turn[:, None], (count, 128)),
    )


def per_device(
    assembly_rhs, source_slot, diagonal_blocks, jacobi_blocks, coupling, neighbor, neighbor_face, orientation
):
    devices, layers = lax.axis_size("blk"), lax.axis_size("reg")
    chips = devices // 2
    jacobi = pl.pallas_call(
        hold_kernel,
        out_shape=shape(ELEMS, DOF, DOF, dtype=BF16),
        in_specs=anywhere(1),
        out_specs=vmem(1)[0],
        scratch_shapes=[pltpu.SemaphoreType.DMA],
        compiler_params=params(8),
        cost_estimate=cost(100000, 2**21),
        name="hold",
    )(in_hbm(jacobi_blocks[0]))
    held_select = [pltpu.VMEM((6 * FDOF, DOF), BF16)]
    diagonal = diagonal_blocks[0]
    coupling = coupling.reshape(6 * ELEMS, FDOF, FDOF)

    rows = jnp.transpose(assembly_rhs, (1, 0, 2))
    rows = pl.pallas_call(
        repeat_kernel,
        out_shape=shape(chips, 1, SLOTS * DOF),
        in_specs=vmem(1),
        out_specs=vmem(1)[0],
        compiler_params=params(8),
        cost_estimate=cost(1000, 2**19),
        name="repeat",
    )(rows)
    same_core = [[2 * chip + core for chip in range(chips)] for core in range(2)]
    same = lax.all_to_all(rows, "blk", 0, 0, axis_index_groups=same_core, tiled=True)
    other = lax.ppermute(same, "blk", [(device, device ^ 1) for device in range(devices)])

    owner = source_slot // SLOTS
    crossed = (owner % 2 != lax.axis_index("blk") % 2).astype(jnp.int32)
    place = jnp.concatenate([owner // 2, source_slot % SLOTS, crossed], axis=0)
    pack, unpack, here, turn = routes(neighbor, neighbor_face, orientation, devices)

    vector = shape(PAD, DOF)
    sent = (shape(devices, 1, WIDTH), shape(PAD, 128), shape(PAD, 128), shape(4 * PAD, 128))

    def exchange(send, up, down):
        below = lax.ppermute(up, "reg", [(i, (i + 1) % layers) for i in range(layers)])
        above = lax.ppermute(down, "reg", [((i + 1) % layers, i) for i in range(layers)])
        return lax.all_to_all(send, "blk", 0, 0, tiled=True), below, above

    def diagonal_part(values):
        return pl.pallas_call(
            diagonal_kernel,
            out_shape=vector,
            in_specs=vmem(1) + anywhere(1),
            out_specs=vmem(1)[0],
            scratch_shapes=[pltpu.VMEM((ELEMS, DOF, DOF), F32), pltpu.SemaphoreType.DMA((ELEMS,))],
            compiler_params=params(16),
            cost_estimate=cost(6 * 4 * 16 * 320 * 320, 4 * 2**20),
            name="diagonal_part",
        )(values, in_hbm(diagonal))

    rhs, values, full0, send, up, down, local = pl.pallas_call(
        first_kernel,
        out_shape=(vector,) * 3 + sent,
        in_specs=[smem()] + vmem(4),
        scratch_shapes=held_select + [pltpu.VMEM((PAD, WINDOW), F32)],
        out_specs=tuple(vmem(7)),
        compiler_params=params(16),
        cost_estimate=cost(6 * 2 * 16 * 480 * 320, 2**21),
        name="first",
    )(place, same, other, jacobi, pack)
    recv, below, above = exchange(send, up, down)
    product = diagonal_part(values)

    first, values, full1, send, up, down, local1 = pl.pallas_call(
        middle_kernel,
        out_shape=(vector,) * 3 + sent,
        in_specs=vmem(11),
        scratch_shapes=held_select,
        out_specs=tuple(vmem(7)),
        compiler_params=params(16),
        cost_estimate=cost(6 * 4 * 16 * 480 * 320, 4 * 2**20),
        name="middle",
    )(product, recv, below, above, local, turn, unpack, here, coupling, pack, jacobi)
    recv, below, above = exchange(send, up, down)
    product = diagonal_part(values)

    second, sums = pl.pallas_call(
        last_kernel,
        out_shape=(vector, shape(layers, 1, 128)),
        in_specs=vmem(11),
        scratch_shapes=held_select,
        out_specs=tuple(vmem(2)),
        compiler_params=params(16),
        cost_estimate=cost(6 * 2 * 16 * 480 * 320, 2**21),
        name="last",
    )(product, recv, below, above, local1, turn, unpack, here, coupling, rhs, first)
    sums = lax.all_to_all(sums, "reg", 0, 0, tiled=True)
    sums = pl.pallas_call(
        spread_kernel,
        out_shape=shape(devices, 1, 128),
        in_specs=vmem(1),
        out_specs=vmem(1)[0],
        compiler_params=params(8),
        cost_estimate=cost(2000, 2**15),
        name="spread",
    )(sums)
    sums = lax.all_to_all(sums, "blk", 0, 0, tiled=True)
    answer, remaining = pl.pallas_call(
        finish_kernel,
        out_shape=(shape(ELEMS, 1, DOF), shape(ELEMS, 1, DOF)),
        in_specs=vmem(6),
        out_specs=tuple(vmem(2)),
        compiler_params=params(8),
        cost_estimate=cost(20000, 2**16),
        name="finish",
    )(sums, rhs, first, second, full0, full1)
    return jnp.transpose(answer, (1, 0, 2)), jnp.transpose(remaining, (1, 0, 2))


def solution(mesh):
    placed = (
        P("reg", "blk", None),
        P("reg", "blk"),
        P("reg", "blk", None, None),
        P("reg", "blk", None, None),
        P("reg", "blk", None, None, None),
        P("blk", None),
        P("blk", None),
        P("blk", None),
    )
    return jax.shard_map(
        per_device,
        mesh=mesh,
        in_specs=placed,
        out_specs=(P("reg", "blk", None), P("reg", "blk", None)),
        check_vma=False,
    )
```

```python
import jax
import jax.numpy as jnp
from jax import lax
from jax.experimental import pallas as pl
from jax.experimental.pallas import tpu as pltpu
from jax.sharding import PartitionSpec as P

NVAR = 5
NQ = 4
DOF = NVAR * NQ**3
FDOF = NVAR * NQ**2
ELEMS = 6
PAD = 8
SLOTS = 10
WINDOW = 384
PER_PAIR = 3
WIDTH = 256
F32 = jnp.float32
BF16 = jnp.bfloat16


def fill_select(select_ref):
    row = lax.broadcasted_iota(jnp.int32, (FDOF, DOF), 0)
    entry = lax.broadcasted_iota(jnp.int32, (FDOF, DOF), 1)
    variable = (row >> 4) << 6
    first, second = (row >> 2) & 3, row & 3
    along_i = variable + (row & 15)
    along_j = variable + (first << 4) + second
    along_k = variable + ((row & 15) << 2)
    last = NQ - 1
    places = (along_i, along_i + 16 * last, along_j, along_j + 4 * last, along_k, along_k + last)
    for face, place in enumerate(places):
        select_ref[face * FDOF : (face + 1) * FDOF, :] = jnp.where(entry == place, 1.0, 0.0).astype(BF16)


def params(megabytes):
    return pltpu.CompilerParams(vmem_limit_bytes=megabytes * 2**20)


def cost(flops, moved):
    return pl.CostEstimate(flops=flops, bytes_accessed=moved, transcendentals=0)


def vmem(count):
    return [pl.BlockSpec(memory_space=pltpu.VMEM)] * count


def anywhere(count):
    return [pl.BlockSpec(memory_space=pl.ANY)] * count


def in_hbm(array):
    return pltpu.with_memory_space_constraint(array, pltpu.HBM)


def smem():
    return pl.BlockSpec(memory_space=pltpu.SMEM)


def mul_t(rows, matrix):
    return lax.dot_general(rows, matrix, (((1,), (1,)), ((), ())), preferred_element_type=F32)


def mul(left, right):
    return lax.dot_general(left, right, (((1,), (0,)), ((), ())), preferred_element_type=F32)


def two_parts(values):
    high = values.astype(BF16)
    low = (values - high.astype(F32)).astype(BF16)
    return high, low


def stacked_parts(values):
    high = values.astype(BF16).astype(F32)
    return jnp.concatenate([high, values - high], axis=0).astype(BF16)


def own_row(result, element):
    row = lax.broadcasted_iota(jnp.int32, result[:PAD].shape, 0)
    return jnp.where(row == element, result[:PAD] + result[PAD:], 0.0)


def high_row(result, element):
    row = lax.broadcasted_iota(jnp.int32, result[:PAD].shape, 0)
    return jnp.where(row == element, result[:PAD], 0.0)


def precondition(vector, jacobi_ref):
    parts = stacked_parts(vector)
    rounded = jnp.zeros((PAD, DOF), F32)
    full = jnp.zeros((PAD, DOF), F32)
    for element in range(ELEMS):
        result = mul_t(parts, jacobi_ref[element])
        rounded = rounded + high_row(result, element)
        full = full + own_row(result, element)
    return rounded, full


def send_traces(values, select_ref, pack_ref, send_ref, up_ref, down_ref, local_ref):
    both = mul_t(stacked_parts(values), select_ref[...])
    traces = both[:PAD] + both[PAD:]
    pad = jnp.zeros((PAD, 128 - FDOF), F32)
    traces = [
        jnp.concatenate([traces[:, FDOF * face : FDOF * (face + 1)], pad], axis=1) for face in range(6)
    ]
    down_ref[...] = traces[4]
    up_ref[...] = traces[5]
    sides = jnp.concatenate(traces[:4], axis=0)
    local_ref[...] = sides
    sides = jnp.concatenate([sides, jnp.zeros((4 * PAD, WIDTH - 128), F32)], axis=1)
    spread = jnp.concatenate(
        [sides] + [pltpu.roll(sides, FDOF * place, 1) for place in range(1, PER_PAIR)], axis=0
    )
    high, low = two_parts(spread)
    send_ref[:, 0, :] = mul(pack_ref[...], high) + mul(pack_ref[...], low)


def repeat_kernel(rows_ref, out_ref):
    flat = jnp.concatenate([rows_ref[slot] for slot in range(SLOTS)], axis=1)
    for chip in range(out_ref.shape[0]):
        out_ref[chip] = flat


def hold_kernel(far_ref, near_ref, semaphore):
    copy = pltpu.make_async_copy(far_ref, near_ref, semaphore)
    copy.start()
    copy.wait()


def first_kernel(
    place_ref, same_ref, other_ref, jacobi_ref, pack_ref,
    rhs_ref, values_ref, full_ref, send_ref, up_ref, down_ref, local_ref,
    select_ref, held_ref,
):
    fill_select(select_ref)
    held_ref[...] = jnp.zeros(held_ref.shape, F32)
    for element in range(ELEMS):
        chip, slot = place_ref[0, element], place_ref[1, element]
        lanes = pl.ds(pl.multiple_of((slot * 5 // 2) * 128, 128), WINDOW)
        window = jnp.where(place_ref[2, element] == 1, other_ref[chip, :, lanes], same_ref[chip, :, lanes])
        turned = pltpu.roll(window, WINDOW - 64, 1)
        held_ref[element : element + 1, :] = jnp.where(slot % 2 == 1, turned, window)
    rhs_ref[...] = held_ref[:, :DOF]
    rounded, full = precondition(rhs_ref[...], jacobi_ref)
    values_ref[...] = rounded
    full_ref[...] = full
    send_traces(rounded, select_ref, pack_ref, send_ref, up_ref, down_ref, local_ref)


def fetch(source_ref, target_ref, semaphores):
    copies = [
        pltpu.make_async_copy(source_ref.at[element], target_ref.at[element], semaphores.at[element])
        for element in range(ELEMS)
    ]
    for copy in copies:
        copy.start()
    return lambda element: copies[element].wait()


def diagonal_kernel(values_ref, diagonal_ref, product_ref, held_ref, semaphores):
    arrive = fetch(diagonal_ref, held_ref, semaphores)
    parts = stacked_parts(values_ref[...])
    total = jnp.zeros((PAD, DOF), F32)
    for element in range(ELEMS):
        arrive(element)
        high, low = two_parts(held_ref[element])
        total = total + own_row(mul_t(parts, high) + mul_t(parts, low), element)
    product_ref[...] = total


def add_neighbors(
    product_ref, recv_ref, below_ref, above_ref, local_ref, turn_ref, unpack_ref, here_ref, coupling_ref,
    select_ref,
):
    high, low = two_parts(recv_ref[:, 0, :])
    arrived = mul(unpack_ref[...], high) + mul(unpack_ref[...], low)
    count = 4 * PAD
    sides = arrived[:count, :128]
    for place in range(1, PER_PAIR):
        rows = arrived[place * count : (place + 1) * count]
        sides = sides + pltpu.roll(rows, WIDTH - FDOF * place, 1)[:, :128]
    high, low = two_parts(local_ref[...])
    sides = sides + mul(here_ref[...], high) + mul(here_ref[...], low)
    lane = lax.broadcasted_iota(jnp.int32, sides.shape, 1)
    step = (lane // 4) % 4
    turned = jnp.where(
        step == 0,
        pltpu.roll(sides, 128 - 12, 1),
        jnp.where(
            step == 1,
            pltpu.roll(sides, 128 - 4, 1),
            jnp.where(step == 2, pltpu.roll(sides, 4, 1), pltpu.roll(sides, 12, 1)),
        ),
    )
    sides = jnp.where(turn_ref[...] == 1, turned, sides)
    traces = [sides[face * PAD : (face + 1) * PAD] for face in range(4)] + [below_ref[...], above_ref[...]]
    parts = [stacked_parts(one[:, :FDOF]) for one in traces]
    terms = [jnp.zeros((PAD, FDOF), F32)] * 6
    for face in range(6):
        blocks = jnp.concatenate([coupling_ref[element * 6 + face] for element in range(ELEMS)], axis=0)
        high, low = two_parts(blocks)
        result = mul_t(parts[face], high) + mul_t(parts[face], low)
        for element in range(ELEMS):
            own = result[:, element * FDOF : (element + 1) * FDOF]
            terms[face] = terms[face] + own_row(own, element)
    total = product_ref[...]
    for face in range(6):
        lifted = mul(stacked_parts(terms[face]), select_ref[face * FDOF : (face + 1) * FDOF, :])
        total = total + lifted[:PAD] + lifted[PAD:]
    return total


def middle_kernel(
    product_ref, recv_ref, below_ref, above_ref, local_ref, turn_ref, unpack_ref, here_ref, coupling_ref,
    pack_ref, jacobi_ref,
    vector_ref, values_ref, full_ref, send_ref, up_ref, down_ref, new_local_ref,
    select_ref,
):
    fill_select(select_ref)
    vector = add_neighbors(
        product_ref, recv_ref, below_ref, above_ref, local_ref, turn_ref, unpack_ref, here_ref, coupling_ref,
        select_ref,
    )
    vector_ref[...] = vector
    rounded, full = precondition(vector, jacobi_ref)
    values_ref[...] = rounded
    full_ref[...] = full
    send_traces(rounded, select_ref, pack_ref, send_ref, up_ref, down_ref, new_local_ref)


def last_kernel(
    product_ref, recv_ref, below_ref, above_ref, local_ref, turn_ref, unpack_ref, here_ref, coupling_ref,
    rhs_ref, first_ref,
    vector_ref, sums_ref,
    select_ref,
):
    fill_select(select_ref)
    second = add_neighbors(
        product_ref, recv_ref, below_ref, above_ref, local_ref, turn_ref, unpack_ref, here_ref, coupling_ref,
        select_ref,
    )
    vector_ref[...] = second
    first, rhs = first_ref[...], rhs_ref[...]
    lane = lax.broadcasted_iota(jnp.int32, (1, 128), 1)
    sums = jnp.zeros((1, 128), F32)
    pairs = ((first, first), (first, second), (second, second), (first, rhs), (second, rhs))
    for place, (one, other) in enumerate(pairs):
        sums = jnp.where(lane == place, jnp.sum(one * other), sums)
    for copy in range(sums_ref.shape[0]):
        sums_ref[copy] = sums


def add_parts(parts_ref):
    totals = [parts_ref[part] for part in range(parts_ref.shape[0])]
    while len(totals) > 1:
        totals = [one + other for one, other in zip(totals[::2], totals[1::2])] + totals[len(totals) // 2 * 2 :]
    return totals[0]


def spread_kernel(parts_ref, sums_ref):
    total = add_parts(parts_ref)
    for copy in range(sums_ref.shape[0]):
        sums_ref[copy] = total


def finish_kernel(parts_ref, rhs_ref, first_ref, second_ref, full0_ref, full1_ref, solution_ref, residual_ref):
    total = add_parts(parts_ref)
    g11, g12, g22, t1, t2 = (total[:, place : place + 1] for place in range(5))
    factor = g12 / g11
    weight2 = (t2 - factor * t1) / (g22 - factor * g12)
    weight1 = (t1 - g12 * weight2) / g11
    answer = weight1 * full0_ref[...] + weight2 * full1_ref[...]
    remaining = rhs_ref[...] - weight1 * first_ref[...] - weight2 * second_ref[...]
    for element in range(ELEMS):
        solution_ref[element] = answer[element : element + 1]
        residual_ref[element] = remaining[element : element + 1]


def shape(*dims, dtype=F32):
    return jax.ShapeDtypeStruct(dims, dtype)


def routes(neighbor, neighbor_face, orientation, devices):
    def sides(table, fill):
        padded = jnp.pad(table.T, ((0, 0), (0, PAD - ELEMS)), constant_values=fill)
        return padded.reshape(-1)

    own = lax.axis_index("blk").astype(jnp.int32)
    near = sides(neighbor, -ELEMS)
    face = sides(neighbor_face, 0)
    turn = sides(orientation, 0)
    count = 4 * PAD
    row = jnp.arange(count, dtype=jnp.int32)
    owner = near // ELEMS
    remote = (owner != own) & (near >= 0)
    local = owner == own
    same = owner[:, None] == owner[None, :]
    own_key = row % PAD * 4 + row // PAD
    near_key = near * 4 + face
    send_place = jnp.sum(same & (own_key[None, :] < own_key[:, None]), axis=1)
    near_place = jnp.sum(same & (near_key[None, :] < near_key[:, None]), axis=1)
    device = jnp.arange(devices, dtype=jnp.int32)
    place = jnp.arange(PER_PAIR, dtype=jnp.int32)
    to = (device[:, None] == owner[None, :]) & remote[None, :]
    pack = to[:, None, :] & (place[None, :, None] == send_place[None, None, :])
    unpack = to.T[None] & (place[:, None, None] == near_place[None, :, None])
    here = local[:, None] & (row[None, :] == (face * PAD + near % ELEMS)[:, None])
    return (
        pack.reshape(devices, PER_PAIR * count).astype(BF16),
        unpack.reshape(PER_PAIR * count, devices).astype(BF16),
        here.astype(BF16),
        jnp.broadcast_to(turn[:, None], (count, 128)),
    )


def per_device(
    assembly_rhs, source_slot, diagonal_blocks, jacobi_blocks, coupling, neighbor, neighbor_face, orientation
):
    devices, layers = lax.axis_size("blk"), lax.axis_size("reg")
    chips = devices // 2
    jacobi = pl.pallas_call(
        hold_kernel,
        out_shape=shape(ELEMS, DOF, DOF, dtype=BF16),
        in_specs=anywhere(1),
        out_specs=vmem(1)[0],
        scratch_shapes=[pltpu.SemaphoreType.DMA],
        compiler_params=params(8),
        cost_estimate=cost(100000, 2**21),
        name="hold",
    )(in_hbm(jacobi_blocks[0]))
    held_select = [pltpu.VMEM((6 * FDOF, DOF), BF16)]
    diagonal = diagonal_blocks[0]
    coupling = coupling.reshape(6 * ELEMS, FDOF, FDOF)

    rows = jnp.transpose(assembly_rhs, (1, 0, 2))
    rows = pl.pallas_call(
        repeat_kernel,
        out_shape=shape(chips, 1, SLOTS * DOF),
        in_specs=vmem(1),
        out_specs=vmem(1)[0],
        compiler_params=params(8),
        cost_estimate=cost(1000, 2**19),
        name="repeat",
    )(rows)
    same_core = [[2 * chip + core for chip in range(chips)] for core in range(2)]
    same = lax.all_to_all(rows, "blk", 0, 0, axis_index_groups=same_core, tiled=True)
    other = lax.ppermute(same, "blk", [(device, device ^ 1) for device in range(devices)])

    owner = source_slot // SLOTS
    crossed = (owner % 2 != lax.axis_index("blk") % 2).astype(jnp.int32)
    place = jnp.concatenate([owner // 2, source_slot % SLOTS, crossed], axis=0)
    pack, unpack, here, turn = routes(neighbor, neighbor_face, orientation, devices)

    vector = shape(PAD, DOF)
    sent = (shape(devices, 1, WIDTH), shape(PAD, 128), shape(PAD, 128), shape(4 * PAD, 128))

    def exchange(send, up, down):
        below = lax.ppermute(up, "reg", [(i, (i + 1) % layers) for i in range(layers)])
        above = lax.ppermute(down, "reg", [((i + 1) % layers, i) for i in range(layers)])
        return lax.all_to_all(send, "blk", 0, 0, tiled=True), below, above

    def diagonal_part(values):
        return pl.pallas_call(
            diagonal_kernel,
            out_shape=vector,
            in_specs=vmem(1) + anywhere(1),
            out_specs=vmem(1)[0],
            scratch_shapes=[pltpu.VMEM((ELEMS, DOF, DOF), F32), pltpu.SemaphoreType.DMA((ELEMS,))],
            compiler_params=params(16),
            cost_estimate=cost(6 * 4 * 16 * 320 * 320, 4 * 2**20),
            name="diagonal_part",
        )(values, in_hbm(diagonal))

    rhs, values, full0, send, up, down, local = pl.pallas_call(
        first_kernel,
        out_shape=(vector,) * 3 + sent,
        in_specs=[smem()] + vmem(4),
        scratch_shapes=held_select + [pltpu.VMEM((PAD, WINDOW), F32)],
        out_specs=tuple(vmem(7)),
        compiler_params=params(16),
        cost_estimate=cost(6 * 2 * 16 * 480 * 320, 2**21),
        name="first",
    )(place, same, other, jacobi, pack)
    recv, below, above = exchange(send, up, down)
    product = diagonal_part(values)

    first, values, full1, send, up, down, local1 = pl.pallas_call(
        middle_kernel,
        out_shape=(vector,) * 3 + sent,
        in_specs=vmem(11),
        scratch_shapes=held_select,
        out_specs=tuple(vmem(7)),
        compiler_params=params(16),
        cost_estimate=cost(6 * 4 * 16 * 480 * 320, 4 * 2**20),
        name="middle",
    )(product, recv, below, above, local, turn, unpack, here, coupling, pack, jacobi)
    recv, below, above = exchange(send, up, down)
    product = diagonal_part(values)

    second, sums = pl.pallas_call(
        last_kernel,
        out_shape=(vector, shape(devices, 1, 128)),
        in_specs=vmem(11),
        scratch_shapes=held_select,
        out_specs=tuple(vmem(2)),
        compiler_params=params(16),
        cost_estimate=cost(6 * 2 * 16 * 480 * 320, 2**21),
        name="last",
    )(product, recv, below, above, local1, turn, unpack, here, coupling, rhs, first)
    sums = lax.all_to_all(sums, "blk", 0, 0, tiled=True)
    sums = pl.pallas_call(
        spread_kernel,
        out_shape=shape(layers, 1, 128),
        in_specs=vmem(1),
        out_specs=vmem(1)[0],
        compiler_params=params(8),
        cost_estimate=cost(2000, 2**15),
        name="spread",
    )(sums)
    sums = lax.all_to_all(sums, "reg", 0, 0, tiled=True)
    answer, remaining = pl.pallas_call(
        finish_kernel,
        out_shape=(shape(ELEMS, 1, DOF), shape(ELEMS, 1, DOF)),
        in_specs=vmem(6),
        out_specs=tuple(vmem(2)),
        compiler_params=params(8),
        cost_estimate=cost(20000, 2**16),
        name="finish",
    )(sums, rhs, first, second, full0, full1)
    return jnp.transpose(answer, (1, 0, 2)), jnp.transpose(remaining, (1, 0, 2))


def solution(mesh):
    placed = (
        P("reg", "blk", None),
        P("reg", "blk"),
        P("reg", "blk", None, None),
        P("reg", "blk", None, None),
        P("reg", "blk", None, None, None),
        P("blk", None),
        P("blk", None),
        P("blk", None),
    )
    return jax.shard_map(
        per_device,
        mesh=mesh,
        in_specs=placed,
        out_specs=(P("reg", "blk", None), P("reg", "blk", None)),
        check_vma=False,
    )
```

```python
import jax
import jax.numpy as jnp
from jax import lax
from jax.experimental import pallas as pl
from jax.experimental.pallas import tpu as pltpu
from jax.sharding import PartitionSpec as P

NVAR = 5
NQ = 4
DOF = NVAR * NQ**3
FDOF = NVAR * NQ**2
ELEMS = 6
PAD = 8
SLOTS = 10
WINDOW = 384
PER_PAIR = 3
WIDTH = 256
F32 = jnp.float32
BF16 = jnp.bfloat16


def fill_select(select_ref):
    row = lax.broadcasted_iota(jnp.int32, (FDOF, DOF), 0)
    entry = lax.broadcasted_iota(jnp.int32, (FDOF, DOF), 1)
    variable = (row >> 4) << 6
    first, second = (row >> 2) & 3, row & 3
    along_i = variable + (row & 15)
    along_j = variable + (first << 4) + second
    along_k = variable + ((row & 15) << 2)
    last = NQ - 1
    places = (along_i, along_i + 16 * last, along_j, along_j + 4 * last, along_k, along_k + last)
    for face, place in enumerate(places):
        select_ref[face * FDOF : (face + 1) * FDOF, :] = jnp.where(entry == place, 1.0, 0.0).astype(BF16)


def params(megabytes):
    return pltpu.CompilerParams(vmem_limit_bytes=megabytes * 2**20)


def cost(flops, moved):
    return pl.CostEstimate(flops=flops, bytes_accessed=moved, transcendentals=0)


def vmem(count):
    return [pl.BlockSpec(memory_space=pltpu.VMEM)] * count


def anywhere(count):
    return [pl.BlockSpec(memory_space=pl.ANY)] * count


def in_hbm(array):
    return pltpu.with_memory_space_constraint(array, pltpu.HBM)


def smem():
    return pl.BlockSpec(memory_space=pltpu.SMEM)


def mul_t(rows, matrix):
    return lax.dot_general(rows, matrix, (((1,), (1,)), ((), ())), preferred_element_type=F32)


def mul(left, right):
    return lax.dot_general(left, right, (((1,), (0,)), ((), ())), preferred_element_type=F32)


def two_parts(values):
    high = values.astype(BF16)
    low = (values - high.astype(F32)).astype(BF16)
    return high, low


def stacked_parts(values):
    high = values.astype(BF16).astype(F32)
    return jnp.concatenate([high, values - high], axis=0).astype(BF16)


def own_row(result, element):
    row = lax.broadcasted_iota(jnp.int32, result[:PAD].shape, 0)
    return jnp.where(row == element, result[:PAD] + result[PAD:], 0.0)


def high_row(result, element):
    row = lax.broadcasted_iota(jnp.int32, result[:PAD].shape, 0)
    return jnp.where(row == element, result[:PAD], 0.0)


def precondition(vector, jacobi_ref):
    parts = stacked_parts(vector)
    rounded = jnp.zeros((PAD, DOF), F32)
    full = jnp.zeros((PAD, DOF), F32)
    for element in range(ELEMS):
        result = mul_t(parts, jacobi_ref[element])
        rounded = rounded + high_row(result, element)
        full = full + own_row(result, element)
    return rounded, full


def send_traces(values, select_ref, pack_ref, send_ref, up_ref, down_ref, local_ref):
    both = mul_t(stacked_parts(values), select_ref[...])
    traces = both[:PAD] + both[PAD:]
    pad = jnp.zeros((PAD, 128 - FDOF), F32)
    traces = [
        jnp.concatenate([traces[:, FDOF * face : FDOF * (face + 1)], pad], axis=1) for face in range(6)
    ]
    down_ref[...] = traces[4]
    up_ref[...] = traces[5]
    sides = jnp.concatenate(traces[:4], axis=0)
    local_ref[...] = sides
    sides = jnp.concatenate([sides, jnp.zeros((4 * PAD, WIDTH - 128), F32)], axis=1)
    spread = jnp.concatenate(
        [sides] + [pltpu.roll(sides, FDOF * place, 1) for place in range(1, PER_PAIR)], axis=0
    )
    high, low = two_parts(spread)
    send_ref[:, 0, :] = mul(pack_ref[...], high) + mul(pack_ref[...], low)


def repeat_kernel(far_ref, out_ref, rows_ref, semaphore):
    copy = pltpu.make_async_copy(far_ref, rows_ref, semaphore)
    copy.start()
    copy.wait()
    flat = jnp.concatenate([rows_ref[slot] for slot in range(SLOTS)], axis=1)
    for chip in range(out_ref.shape[0]):
        out_ref[chip] = flat


def hold_kernel(far_ref, near_ref, semaphore):
    copy = pltpu.make_async_copy(far_ref, near_ref, semaphore)
    copy.start()
    copy.wait()


def first_kernel(
    place_ref, same_ref, other_ref, jacobi_ref, pack_ref,
    rhs_ref, values_ref, full_ref, send_ref, up_ref, down_ref, local_ref,
    select_ref, held_ref,
):
    fill_select(select_ref)
    held_ref[...] = jnp.zeros(held_ref.shape, F32)
    for element in range(ELEMS):
        chip, slot = place_ref[0, element], place_ref[1, element]
        lanes = pl.ds(pl.multiple_of((slot * 5 // 2) * 128, 128), WINDOW)
        window = jnp.where(place_ref[2, element] == 1, other_ref[chip, :, lanes], same_ref[chip, :, lanes])
        turned = pltpu.roll(window, WINDOW - 64, 1)
        held_ref[element : element + 1, :] = jnp.where(slot % 2 == 1, turned, window)
    rhs_ref[...] = held_ref[:, :DOF]
    rounded, full = precondition(rhs_ref[...], jacobi_ref)
    values_ref[...] = rounded
    full_ref[...] = full
    send_traces(rounded, select_ref, pack_ref, send_ref, up_ref, down_ref, local_ref)


def fetch(source_ref, target_ref, semaphores):
    copies = [
        pltpu.make_async_copy(source_ref.at[element], target_ref.at[element], semaphores.at[element])
        for element in range(ELEMS)
    ]
    for copy in copies:
        copy.start()
    return lambda element: copies[element].wait()


def diagonal_kernel(values_ref, diagonal_ref, product_ref, held_ref, semaphores):
    arrive = fetch(diagonal_ref, held_ref, semaphores)
    parts = stacked_parts(values_ref[...])
    total = jnp.zeros((PAD, DOF), F32)
    for element in range(ELEMS):
        arrive(element)
        high, low = two_parts(held_ref[element])
        total = total + own_row(mul_t(parts, high) + mul_t(parts, low), element)
    product_ref[...] = total


def add_neighbors(
    product_ref, recv_ref, below_ref, above_ref, local_ref, turn_ref, unpack_ref, here_ref, coupling_ref,
    select_ref,
):
    high, low = two_parts(recv_ref[:, 0, :])
    arrived = mul(unpack_ref[...], high) + mul(unpack_ref[...], low)
    count = 4 * PAD
    sides = arrived[:count, :128]
    for place in range(1, PER_PAIR):
        rows = arrived[place * count : (place + 1) * count]
        sides = sides + pltpu.roll(rows, WIDTH - FDOF * place, 1)[:, :128]
    high, low = two_parts(local_ref[...])
    sides = sides + mul(here_ref[...], high) + mul(here_ref[...], low)
    lane = lax.broadcasted_iota(jnp.int32, sides.shape, 1)
    step = (lane // 4) % 4
    turned = jnp.where(
        step == 0,
        pltpu.roll(sides, 128 - 12, 1),
        jnp.where(
            step == 1,
            pltpu.roll(sides, 128 - 4, 1),
            jnp.where(step == 2, pltpu.roll(sides, 4, 1), pltpu.roll(sides, 12, 1)),
        ),
    )
    sides = jnp.where(turn_ref[...] == 1, turned, sides)
    traces = [sides[face * PAD : (face + 1) * PAD] for face in range(4)] + [below_ref[...], above_ref[...]]
    parts = [stacked_parts(one[:, :FDOF]) for one in traces]
    terms = [jnp.zeros((PAD, FDOF), F32)] * 6
    for face in range(6):
        blocks = jnp.concatenate([coupling_ref[element * 6 + face] for element in range(ELEMS)], axis=0)
        high, low = two_parts(blocks)
        result = mul_t(parts[face], high) + mul_t(parts[face], low)
        for element in range(ELEMS):
            own = result[:, element * FDOF : (element + 1) * FDOF]
            terms[face] = terms[face] + own_row(own, element)
    total = product_ref[...]
    for face in range(6):
        lifted = mul(stacked_parts(terms[face]), select_ref[face * FDOF : (face + 1) * FDOF, :])
        total = total + lifted[:PAD] + lifted[PAD:]
    return total


def middle_kernel(
    product_ref, recv_ref, below_ref, above_ref, local_ref, turn_ref, unpack_ref, here_ref, coupling_ref,
    pack_ref, jacobi_ref,
    vector_ref, values_ref, full_ref, send_ref, up_ref, down_ref, new_local_ref,
    select_ref,
):
    fill_select(select_ref)
    vector = add_neighbors(
        product_ref, recv_ref, below_ref, above_ref, local_ref, turn_ref, unpack_ref, here_ref, coupling_ref,
        select_ref,
    )
    vector_ref[...] = vector
    rounded, full = precondition(vector, jacobi_ref)
    values_ref[...] = rounded
    full_ref[...] = full
    send_traces(rounded, select_ref, pack_ref, send_ref, up_ref, down_ref, new_local_ref)


def last_kernel(
    product_ref, recv_ref, below_ref, above_ref, local_ref, turn_ref, unpack_ref, here_ref, coupling_ref,
    rhs_ref, first_ref,
    vector_ref, sums_ref,
    select_ref,
):
    fill_select(select_ref)
    second = add_neighbors(
        product_ref, recv_ref, below_ref, above_ref, local_ref, turn_ref, unpack_ref, here_ref, coupling_ref,
        select_ref,
    )
    vector_ref[...] = second
    first, rhs = first_ref[...], rhs_ref[...]
    lane = lax.broadcasted_iota(jnp.int32, (1, 128), 1)
    sums = jnp.zeros((1, 128), F32)
    pairs = ((first, first), (first, second), (second, second), (first, rhs), (second, rhs))
    for place, (one, other) in enumerate(pairs):
        by_lane = jnp.sum(one * other, axis=0, keepdims=True)
        sums = jnp.where(lane == place, jnp.sum(by_lane, axis=1, keepdims=True), sums)
    for copy in range(sums_ref.shape[0]):
        sums_ref[copy] = sums


def add_parts(parts_ref):
    totals = [parts_ref[part] for part in range(parts_ref.shape[0])]
    while len(totals) > 1:
        totals = [one + other for one, other in zip(totals[::2], totals[1::2])] + totals[len(totals) // 2 * 2 :]
    return totals[0]


def spread_kernel(parts_ref, sums_ref):
    total = add_parts(parts_ref)
    for copy in range(sums_ref.shape[0]):
        sums_ref[copy] = total


def finish_kernel(parts_ref, rhs_ref, first_ref, second_ref, full0_ref, full1_ref, solution_ref, residual_ref):
    total = add_parts(parts_ref)
    g11, g12, g22, t1, t2 = (total[:, place : place + 1] for place in range(5))
    factor = g12 / g11
    weight2 = (t2 - factor * t1) / (g22 - factor * g12)
    weight1 = (t1 - g12 * weight2) / g11
    answer = weight1 * full0_ref[...] + weight2 * full1_ref[...]
    remaining = rhs_ref[...] - weight1 * first_ref[...] - weight2 * second_ref[...]
    for element in range(ELEMS):
        solution_ref[element] = answer[element : element + 1]
        residual_ref[element] = remaining[element : element + 1]


def shape(*dims, dtype=F32):
    return jax.ShapeDtypeStruct(dims, dtype)


def routes(neighbor, neighbor_face, orientation, devices):
    def sides(table, fill):
        padded = jnp.pad(table.T, ((0, 0), (0, PAD - ELEMS)), constant_values=fill)
        return padded.reshape(-1)

    own = lax.axis_index("blk").astype(jnp.int32)
    near = sides(neighbor, -ELEMS)
    face = sides(neighbor_face, 0)
    turn = sides(orientation, 0)
    count = 4 * PAD
    row = jnp.arange(count, dtype=jnp.int32)
    owner = near // ELEMS
    remote = (owner != own) & (near >= 0)
    local = owner == own
    same = owner[:, None] == owner[None, :]
    own_key = row % PAD * 4 + row // PAD
    near_key = near * 4 + face
    send_place = jnp.sum(same & (own_key[None, :] < own_key[:, None]), axis=1)
    near_place = jnp.sum(same & (near_key[None, :] < near_key[:, None]), axis=1)
    device = jnp.arange(devices, dtype=jnp.int32)
    place = jnp.arange(PER_PAIR, dtype=jnp.int32)
    to = (device[:, None] == owner[None, :]) & remote[None, :]
    pack = to[:, None, :] & (place[None, :, None] == send_place[None, None, :])
    unpack = to.T[None] & (place[:, None, None] == near_place[None, :, None])
    here = local[:, None] & (row[None, :] == (face * PAD + near % ELEMS)[:, None])
    return (
        pack.reshape(devices, PER_PAIR * count).astype(BF16),
        unpack.reshape(PER_PAIR * count, devices).astype(BF16),
        here.astype(BF16),
        jnp.broadcast_to(turn[:, None], (count, 128)),
    )


def per_device(
    assembly_rhs, source_slot, diagonal_blocks, jacobi_blocks, coupling, neighbor, neighbor_face, orientation
):
    devices, layers = lax.axis_size("blk"), lax.axis_size("reg")
    chips = devices // 2
    jacobi = pl.pallas_call(
        hold_kernel,
        out_shape=shape(ELEMS, DOF, DOF, dtype=BF16),
        in_specs=anywhere(1),
        out_specs=vmem(1)[0],
        scratch_shapes=[pltpu.SemaphoreType.DMA],
        compiler_params=params(8),
        cost_estimate=cost(100000, 2**21),
        name="hold",
    )(in_hbm(jacobi_blocks[0]))
    held_select = [pltpu.VMEM((6 * FDOF, DOF), BF16)]
    diagonal = diagonal_blocks[0]
    coupling = coupling.reshape(6 * ELEMS, FDOF, FDOF)

    rows = jnp.transpose(assembly_rhs, (1, 0, 2))
    rows = pl.pallas_call(
        repeat_kernel,
        out_shape=shape(chips, 1, SLOTS * DOF),
        in_specs=anywhere(1),
        out_specs=vmem(1)[0],
        scratch_shapes=[pltpu.VMEM((SLOTS, 1, DOF), F32), pltpu.SemaphoreType.DMA],
        compiler_params=params(8),
        cost_estimate=cost(1000, 2**19),
        name="repeat",
    )(in_hbm(rows))
    same_core = [[2 * chip + core for chip in range(chips)] for core in range(2)]
    same = lax.all_to_all(rows, "blk", 0, 0, axis_index_groups=same_core, tiled=True)
    other = lax.ppermute(same, "blk", [(device, device ^ 1) for device in range(devices)])

    owner = source_slot // SLOTS
    crossed = (owner % 2 != lax.axis_index("blk") % 2).astype(jnp.int32)
    place = jnp.concatenate([owner // 2, source_slot % SLOTS, crossed], axis=0)
    pack, unpack, here, turn = routes(neighbor, neighbor_face, orientation, devices)

    vector = shape(PAD, DOF)
    sent = (shape(devices, 1, WIDTH), shape(PAD, 128), shape(PAD, 128), shape(4 * PAD, 128))

    def exchange(send, up, down):
        below = lax.ppermute(up, "reg", [(i, (i + 1) % layers) for i in range(layers)])
        above = lax.ppermute(down, "reg", [((i + 1) % layers, i) for i in range(layers)])
        return lax.all_to_all(send, "blk", 0, 0, tiled=True), below, above

    def diagonal_part(values):
        return pl.pallas_call(
            diagonal_kernel,
            out_shape=vector,
            in_specs=vmem(1) + anywhere(1),
            out_specs=vmem(1)[0],
            scratch_shapes=[pltpu.VMEM((ELEMS, DOF, DOF), F32), pltpu.SemaphoreType.DMA((ELEMS,))],
            compiler_params=params(16),
            cost_estimate=cost(6 * 4 * 16 * 320 * 320, 4 * 2**20),
            name="diagonal_part",
        )(values, in_hbm(diagonal))

    rhs, values, full0, send, up, down, local = pl.pallas_call(
        first_kernel,
        out_shape=(vector,) * 3 + sent,
        in_specs=[smem()] + vmem(4),
        scratch_shapes=held_select + [pltpu.VMEM((PAD, WINDOW), F32)],
        out_specs=tuple(vmem(7)),
        compiler_params=params(16),
        cost_estimate=cost(6 * 2 * 16 * 480 * 320, 2**21),
        name="first",
    )(place, same, other, jacobi, pack)
    recv, below, above = exchange(send, up, down)
    product = diagonal_part(values)

    first, values, full1, send, up, down, local1 = pl.pallas_call(
        middle_kernel,
        out_shape=(vector,) * 3 + sent,
        in_specs=vmem(11),
        scratch_shapes=held_select,
        out_specs=tuple(vmem(7)),
        compiler_params=params(16),
        cost_estimate=cost(6 * 4 * 16 * 480 * 320, 4 * 2**20),
        name="middle",
    )(product, recv, below, above, local, turn, unpack, here, coupling, pack, jacobi)
    recv, below, above = exchange(send, up, down)
    product = diagonal_part(values)

    second, sums = pl.pallas_call(
        last_kernel,
        out_shape=(vector, shape(devices, 1, 128)),
        in_specs=vmem(11),
        scratch_shapes=held_select,
        out_specs=tuple(vmem(2)),
        compiler_params=params(16),
        cost_estimate=cost(6 * 2 * 16 * 480 * 320, 2**21),
        name="last",
    )(product, recv, below, above, local1, turn, unpack, here, coupling, rhs, first)
    sums = lax.all_to_all(sums, "blk", 0, 0, tiled=True)
    sums = pl.pallas_call(
        spread_kernel,
        out_shape=shape(layers, 1, 128),
        in_specs=vmem(1),
        out_specs=vmem(1)[0],
        compiler_params=params(8),
        cost_estimate=cost(2000, 2**15),
        name="spread",
    )(sums)
    sums = lax.all_to_all(sums, "reg", 0, 0, tiled=True)
    answer, remaining = pl.pallas_call(
        finish_kernel,
        out_shape=(shape(ELEMS, 1, DOF), shape(ELEMS, 1, DOF)),
        in_specs=vmem(6),
        out_specs=tuple(vmem(2)),
        compiler_params=params(8),
        cost_estimate=cost(20000, 2**16),
        name="finish",
    )(sums, rhs, first, second, full0, full1)
    return jnp.transpose(answer, (1, 0, 2)), jnp.transpose(remaining, (1, 0, 2))


def solution(mesh):
    placed = (
        P("reg", "blk", None),
        P("reg", "blk"),
        P("reg", "blk", None, None),
        P("reg", "blk", None, None),
        P("reg", "blk", None, None, None),
        P("blk", None),
        P("blk", None),
        P("blk", None),
    )
    return jax.shard_map(
        per_device,
        mesh=mesh,
        in_specs=placed,
        out_specs=(P("reg", "blk", None), P("reg", "blk", None)),
        check_vma=False,
    )
```

```python
import jax
import jax.numpy as jnp
from jax import lax
from jax.experimental import pallas as pl
from jax.experimental.pallas import tpu as pltpu
from jax.sharding import PartitionSpec as P

NVAR = 5
NQ = 4
DOF = NVAR * NQ**3
FDOF = NVAR * NQ**2
ELEMS = 6
PAD = 8
SLOTS = 10
WINDOW = 384
PER_PAIR = 3
WIDTH = 256
F32 = jnp.float32
BF16 = jnp.bfloat16


def fill_select(select_ref):
    row = lax.broadcasted_iota(jnp.int32, (FDOF, DOF), 0)
    entry = lax.broadcasted_iota(jnp.int32, (FDOF, DOF), 1)
    variable = (row >> 4) << 6
    first, second = (row >> 2) & 3, row & 3
    along_i = variable + (row & 15)
    along_j = variable + (first << 4) + second
    along_k = variable + ((row & 15) << 2)
    last = NQ - 1
    places = (along_i, along_i + 16 * last, along_j, along_j + 4 * last, along_k, along_k + last)
    for face, place in enumerate(places):
        select_ref[face * FDOF : (face + 1) * FDOF, :] = jnp.where(entry == place, 1.0, 0.0).astype(BF16)


def params(megabytes):
    return pltpu.CompilerParams(vmem_limit_bytes=megabytes * 2**20)


def cost(flops, moved):
    return pl.CostEstimate(flops=flops, bytes_accessed=moved, transcendentals=0)


def vmem(count):
    return [pl.BlockSpec(memory_space=pltpu.VMEM)] * count


def anywhere(count):
    return [pl.BlockSpec(memory_space=pl.ANY)] * count


def in_hbm(array):
    return pltpu.with_memory_space_constraint(array, pltpu.HBM)


def smem():
    return pl.BlockSpec(memory_space=pltpu.SMEM)


def mul_t(rows, matrix):
    return lax.dot_general(rows, matrix, (((1,), (1,)), ((), ())), preferred_element_type=F32)


def mul(left, right):
    return lax.dot_general(left, right, (((1,), (0,)), ((), ())), preferred_element_type=F32)


def two_parts(values):
    high = values.astype(BF16)
    low = (values - high.astype(F32)).astype(BF16)
    return high, low


def stacked_parts(values):
    high = values.astype(BF16).astype(F32)
    return jnp.concatenate([high, values - high], axis=0).astype(BF16)


def own_row(result, element):
    row = lax.broadcasted_iota(jnp.int32, result[:PAD].shape, 0)
    return jnp.where(row == element, result[:PAD] + result[PAD:], 0.0)


def high_row(result, element):
    row = lax.broadcasted_iota(jnp.int32, result[:PAD].shape, 0)
    return jnp.where(row == element, result[:PAD], 0.0)


def precondition(vector, jacobi_ref):
    parts = stacked_parts(vector)
    rounded = jnp.zeros((PAD, DOF), F32)
    full = jnp.zeros((PAD, DOF), F32)
    for element in range(ELEMS):
        result = mul_t(parts, jacobi_ref[element])
        rounded = rounded + high_row(result, element)
        full = full + own_row(result, element)
    return rounded, full


def send_traces(values, select_ref, pack_ref, send_ref, up_ref, down_ref, local_ref):
    both = mul_t(stacked_parts(values), select_ref[...])
    traces = both[:PAD] + both[PAD:]
    pad = jnp.zeros((PAD, 128 - FDOF), F32)
    traces = [
        jnp.concatenate([traces[:, FDOF * face : FDOF * (face + 1)], pad], axis=1) for face in range(6)
    ]
    down_ref[...] = traces[4]
    up_ref[...] = traces[5]
    sides = jnp.concatenate(traces[:4], axis=0)
    local_ref[...] = sides
    sides = jnp.concatenate([sides, jnp.zeros((4 * PAD, WIDTH - 128), F32)], axis=1)
    spread = jnp.concatenate(
        [sides] + [pltpu.roll(sides, FDOF * place, 1) for place in range(1, PER_PAIR)], axis=0
    )
    high, low = two_parts(spread)
    send_ref[:, 0, :] = mul(pack_ref[...], high) + mul(pack_ref[...], low)


def repeat_kernel(far_ref, out_ref, rows_ref, semaphore):
    copy = pltpu.make_async_copy(far_ref, rows_ref, semaphore)
    copy.start()
    copy.wait()
    flat = jnp.concatenate([rows_ref[slot] for slot in range(SLOTS)], axis=1)
    for chip in range(out_ref.shape[0]):
        out_ref[chip] = flat


def hold_kernel(far_ref, near_ref, semaphore):
    copy = pltpu.make_async_copy(far_ref, near_ref, semaphore)
    copy.start()
    copy.wait()


def first_kernel(
    place_ref, same_ref, other_ref, jacobi_ref, pack_ref,
    rhs_ref, values_ref, full_ref, send_ref, up_ref, down_ref, local_ref,
    select_ref, held_ref,
):
    fill_select(select_ref)
    held_ref[...] = jnp.zeros(held_ref.shape, F32)
    for element in range(ELEMS):
        chip, slot = place_ref[0, element], place_ref[1, element]
        lanes = pl.ds(pl.multiple_of((slot * 5 // 2) * 128, 128), WINDOW)
        window = jnp.where(place_ref[2, element] == 1, other_ref[chip, :, lanes], same_ref[chip, :, lanes])
        turned = pltpu.roll(window, WINDOW - 64, 1)
        held_ref[element : element + 1, :] = jnp.where(slot % 2 == 1, turned, window)
    rhs_ref[...] = held_ref[:, :DOF]
    rounded, full = precondition(rhs_ref[...], jacobi_ref)
    values_ref[...] = rounded
    full_ref[...] = full
    send_traces(rounded, select_ref, pack_ref, send_ref, up_ref, down_ref, local_ref)


def fetch(source_ref, target_ref, semaphores):
    copies = [
        pltpu.make_async_copy(source_ref.at[element], target_ref.at[element], semaphores.at[element])
        for element in range(ELEMS)
    ]
    for copy in copies:
        copy.start()
    return lambda element: copies[element].wait()


def diagonal_kernel(values_ref, diagonal_ref, product_ref, held_ref, semaphores):
    arrive = fetch(diagonal_ref, held_ref, semaphores)
    parts = stacked_parts(values_ref[...])
    total = jnp.zeros((PAD, DOF), F32)
    for element in range(ELEMS):
        arrive(element)
        high, low = two_parts(held_ref[element])
        both = mul_t(parts, jnp.concatenate([high, low], axis=0))
        total = total + own_row(both[:, :DOF] + both[:, DOF:], element)
    product_ref[...] = total


def add_neighbors(
    product_ref, recv_ref, below_ref, above_ref, local_ref, turn_ref, unpack_ref, here_ref, coupling_ref,
    select_ref,
):
    high, low = two_parts(recv_ref[:, 0, :])
    arrived = mul(unpack_ref[...], high) + mul(unpack_ref[...], low)
    count = 4 * PAD
    sides = arrived[:count, :128]
    for place in range(1, PER_PAIR):
        rows = arrived[place * count : (place + 1) * count]
        sides = sides + pltpu.roll(rows, WIDTH - FDOF * place, 1)[:, :128]
    high, low = two_parts(local_ref[...])
    sides = sides + mul(here_ref[...], high) + mul(here_ref[...], low)
    lane = lax.broadcasted_iota(jnp.int32, sides.shape, 1)
    step = (lane // 4) % 4
    turned = jnp.where(
        step == 0,
        pltpu.roll(sides, 128 - 12, 1),
        jnp.where(
            step == 1,
            pltpu.roll(sides, 128 - 4, 1),
            jnp.where(step == 2, pltpu.roll(sides, 4, 1), pltpu.roll(sides, 12, 1)),
        ),
    )
    sides = jnp.where(turn_ref[...] == 1, turned, sides)
    traces = [sides[face * PAD : (face + 1) * PAD] for face in range(4)] + [below_ref[...], above_ref[...]]
    parts = [stacked_parts(one[:, :FDOF]) for one in traces]
    terms = [jnp.zeros((PAD, FDOF), F32)] * 6
    for face in range(6):
        blocks = jnp.concatenate([coupling_ref[element * 6 + face] for element in range(ELEMS)], axis=0)
        high, low = two_parts(blocks)
        result = mul_t(parts[face], high) + mul_t(parts[face], low)
        for element in range(ELEMS):
            own = result[:, element * FDOF : (element + 1) * FDOF]
            terms[face] = terms[face] + own_row(own, element)
    total = product_ref[...]
    for face in range(6):
        lifted = mul(stacked_parts(terms[face]), select_ref[face * FDOF : (face + 1) * FDOF, :])
        total = total + lifted[:PAD] + lifted[PAD:]
    return total


def middle_kernel(
    product_ref, recv_ref, below_ref, above_ref, local_ref, turn_ref, unpack_ref, here_ref, coupling_ref,
    pack_ref, jacobi_ref,
    vector_ref, values_ref, full_ref, send_ref, up_ref, down_ref, new_local_ref,
    select_ref,
):
    fill_select(select_ref)
    vector = add_neighbors(
        product_ref, recv_ref, below_ref, above_ref, local_ref, turn_ref, unpack_ref, here_ref, coupling_ref,
        select_ref,
    )
    vector_ref[...] = vector
    rounded, full = precondition(vector, jacobi_ref)
    values_ref[...] = rounded
    full_ref[...] = full
    send_traces(rounded, select_ref, pack_ref, send_ref, up_ref, down_ref, new_local_ref)


def last_kernel(
    product_ref, recv_ref, below_ref, above_ref, local_ref, turn_ref, unpack_ref, here_ref, coupling_ref,
    rhs_ref, first_ref,
    vector_ref, sums_ref,
    select_ref,
):
    fill_select(select_ref)
    second = add_neighbors(
        product_ref, recv_ref, below_ref, above_ref, local_ref, turn_ref, unpack_ref, here_ref, coupling_ref,
        select_ref,
    )
    vector_ref[...] = second
    first, rhs = first_ref[...], rhs_ref[...]
    lane = lax.broadcasted_iota(jnp.int32, (1, 128), 1)
    sums = jnp.zeros((1, 128), F32)
    pairs = ((first, first), (first, second), (second, second), (first, rhs), (second, rhs))
    for place, (one, other) in enumerate(pairs):
        by_lane = jnp.sum(one * other, axis=0, keepdims=True)
        sums = jnp.where(lane == place, jnp.sum(by_lane, axis=1, keepdims=True), sums)
    for copy in range(sums_ref.shape[0]):
        sums_ref[copy] = sums


def add_parts(parts_ref):
    totals = [parts_ref[part] for part in range(parts_ref.shape[0])]
    while len(totals) > 1:
        totals = [one + other for one, other in zip(totals[::2], totals[1::2])] + totals[len(totals) // 2 * 2 :]
    return totals[0]


def spread_kernel(parts_ref, sums_ref):
    total = add_parts(parts_ref)
    for copy in range(sums_ref.shape[0]):
        sums_ref[copy] = total


def finish_kernel(parts_ref, rhs_ref, first_ref, second_ref, full0_ref, full1_ref, solution_ref, residual_ref):
    total = add_parts(parts_ref)
    g11, g12, g22, t1, t2 = (total[:, place : place + 1] for place in range(5))
    factor = g12 / g11
    weight2 = (t2 - factor * t1) / (g22 - factor * g12)
    weight1 = (t1 - g12 * weight2) / g11
    answer = weight1 * full0_ref[...] + weight2 * full1_ref[...]
    remaining = rhs_ref[...] - weight1 * first_ref[...] - weight2 * second_ref[...]
    for element in range(ELEMS):
        solution_ref[element] = answer[element : element + 1]
        residual_ref[element] = remaining[element : element + 1]


def shape(*dims, dtype=F32):
    return jax.ShapeDtypeStruct(dims, dtype)


def routes(neighbor, neighbor_face, orientation, devices):
    def sides(table, fill):
        padded = jnp.pad(table.T, ((0, 0), (0, PAD - ELEMS)), constant_values=fill)
        return padded.reshape(-1)

    own = lax.axis_index("blk").astype(jnp.int32)
    near = sides(neighbor, -ELEMS)
    face = sides(neighbor_face, 0)
    turn = sides(orientation, 0)
    count = 4 * PAD
    row = jnp.arange(count, dtype=jnp.int32)
    owner = near // ELEMS
    remote = (owner != own) & (near >= 0)
    local = owner == own
    same = owner[:, None] == owner[None, :]
    own_key = row % PAD * 4 + row // PAD
    near_key = near * 4 + face
    send_place = jnp.sum(same & (own_key[None, :] < own_key[:, None]), axis=1)
    near_place = jnp.sum(same & (near_key[None, :] < near_key[:, None]), axis=1)
    device = jnp.arange(devices, dtype=jnp.int32)
    place = jnp.arange(PER_PAIR, dtype=jnp.int32)
    to = (device[:, None] == owner[None, :]) & remote[None, :]
    pack = to[:, None, :] & (place[None, :, None] == send_place[None, None, :])
    unpack = to.T[None] & (place[:, None, None] == near_place[None, :, None])
    here = local[:, None] & (row[None, :] == (face * PAD + near % ELEMS)[:, None])
    return (
        pack.reshape(devices, PER_PAIR * count).astype(BF16),
        unpack.reshape(PER_PAIR * count, devices).astype(BF16),
        here.astype(BF16),
        jnp.broadcast_to(turn[:, None], (count, 128)),
    )


def per_device(
    assembly_rhs, source_slot, diagonal_blocks, jacobi_blocks, coupling, neighbor, neighbor_face, orientation
):
    devices, layers = lax.axis_size("blk"), lax.axis_size("reg")
    chips = devices // 2
    jacobi = pl.pallas_call(
        hold_kernel,
        out_shape=shape(ELEMS, DOF, DOF, dtype=BF16),
        in_specs=anywhere(1),
        out_specs=vmem(1)[0],
        scratch_shapes=[pltpu.SemaphoreType.DMA],
        compiler_params=params(8),
        cost_estimate=cost(100000, 2**21),
        name="hold",
    )(in_hbm(jacobi_blocks[0]))
    held_select = [pltpu.VMEM((6 * FDOF, DOF), BF16)]
    diagonal = diagonal_blocks[0]
    coupling = coupling.reshape(6 * ELEMS, FDOF, FDOF)

    rows = jnp.transpose(assembly_rhs, (1, 0, 2))
    rows = pl.pallas_call(
        repeat_kernel,
        out_shape=shape(chips, 1, SLOTS * DOF),
        in_specs=anywhere(1),
        out_specs=vmem(1)[0],
        scratch_shapes=[pltpu.VMEM((SLOTS, 1, DOF), F32), pltpu.SemaphoreType.DMA],
        compiler_params=params(8),
        cost_estimate=cost(1000, 2**19),
        name="repeat",
    )(in_hbm(rows))
    same_core = [[2 * chip + core for chip in range(chips)] for core in range(2)]
    same = lax.all_to_all(rows, "blk", 0, 0, axis_index_groups=same_core, tiled=True)
    other = lax.ppermute(same, "blk", [(device, device ^ 1) for device in range(devices)])

    owner = source_slot // SLOTS
    crossed = (owner % 2 != lax.axis_index("blk") % 2).astype(jnp.int32)
    place = jnp.concatenate([owner // 2, source_slot % SLOTS, crossed], axis=0)
    pack, unpack, here, turn = routes(neighbor, neighbor_face, orientation, devices)

    vector = shape(PAD, DOF)
    sent = (shape(devices, 1, WIDTH), shape(PAD, 128), shape(PAD, 128), shape(4 * PAD, 128))

    def exchange(send, up, down):
        below = lax.ppermute(up, "reg", [(i, (i + 1) % layers) for i in range(layers)])
        above = lax.ppermute(down, "reg", [((i + 1) % layers, i) for i in range(layers)])
        return lax.all_to_all(send, "blk", 0, 0, tiled=True), below, above

    def diagonal_part(values):
        return pl.pallas_call(
            diagonal_kernel,
            out_shape=vector,
            in_specs=vmem(1) + anywhere(1),
            out_specs=vmem(1)[0],
            scratch_shapes=[pltpu.VMEM((ELEMS, DOF, DOF), F32), pltpu.SemaphoreType.DMA((ELEMS,))],
            compiler_params=params(16),
            cost_estimate=cost(6 * 4 * 16 * 320 * 320, 4 * 2**20),
            name="diagonal_part",
        )(values, in_hbm(diagonal))

    rhs, values, full0, send, up, down, local = pl.pallas_call(
        first_kernel,
        out_shape=(vector,) * 3 + sent,
        in_specs=[smem()] + vmem(4),
        scratch_shapes=held_select + [pltpu.VMEM((PAD, WINDOW), F32)],
        out_specs=tuple(vmem(7)),
        compiler_params=params(16),
        cost_estimate=cost(6 * 2 * 16 * 480 * 320, 2**21),
        name="first",
    )(place, same, other, jacobi, pack)
    recv, below, above = exchange(send, up, down)
    product = diagonal_part(values)

    first, values, full1, send, up, down, local1 = pl.pallas_call(
        middle_kernel,
        out_shape=(vector,) * 3 + sent,
        in_specs=vmem(11),
        scratch_shapes=held_select,
        out_specs=tuple(vmem(7)),
        compiler_params=params(16),
        cost_estimate=cost(6 * 4 * 16 * 480 * 320, 4 * 2**20),
        name="middle",
    )(product, recv, below, above, local, turn, unpack, here, coupling, pack, jacobi)
    recv, below, above = exchange(send, up, down)
    product = diagonal_part(values)

    second, sums = pl.pallas_call(
        last_kernel,
        out_shape=(vector, shape(devices, 1, 128)),
        in_specs=vmem(11),
        scratch_shapes=held_select,
        out_specs=tuple(vmem(2)),
        compiler_params=params(16),
        cost_estimate=cost(6 * 2 * 16 * 480 * 320, 2**21),
        name="last",
    )(product, recv, below, above, local1, turn, unpack, here, coupling, rhs, first)
    sums = lax.all_to_all(sums, "blk", 0, 0, tiled=True)
    sums = pl.pallas_call(
        spread_kernel,
        out_shape=shape(layers, 1, 128),
        in_specs=vmem(1),
        out_specs=vmem(1)[0],
        compiler_params=params(8),
        cost_estimate=cost(2000, 2**15),
        name="spread",
    )(sums)
    sums = lax.all_to_all(sums, "reg", 0, 0, tiled=True)
    answer, remaining = pl.pallas_call(
        finish_kernel,
        out_shape=(shape(ELEMS, 1, DOF), shape(ELEMS, 1, DOF)),
        in_specs=vmem(6),
        out_specs=tuple(vmem(2)),
        compiler_params=params(8),
        cost_estimate=cost(20000, 2**16),
        name="finish",
    )(sums, rhs, first, second, full0, full1)
    return jnp.transpose(answer, (1, 0, 2)), jnp.transpose(remaining, (1, 0, 2))


def solution(mesh):
    placed = (
        P("reg", "blk", None),
        P("reg", "blk"),
        P("reg", "blk", None, None),
        P("reg", "blk", None, None),
        P("reg", "blk", None, None, None),
        P("blk", None),
        P("blk", None),
        P("blk", None),
    )
    return jax.shard_map(
        per_device,
        mesh=mesh,
        in_specs=placed,
        out_specs=(P("reg", "blk", None), P("reg", "blk", None)),
        check_vma=False,
    )
```
